1024 devices in a mesh: fsdp: 64 (over y, x, core), expert: 16 (over z).
Axes of the slice: x: 4, y: 8, z: 16, core: 2. Of those that a mesh axis runs over, the one named last changes fastest.
Arguments:
- deltas: bfloat16 [1024, 128, 128], P(('fsdp', 'expert')), may hold values from -6 to 6
- scales: bfloat16 [1024], P(('fsdp', 'expert')), may hold values from 0.049804688 to 0.5
- held_block: int32 [1024], P(('fsdp', 'expert')), may hold values from -1 to 223, as said below
- block_dest: int32 [224], replicated, may hold values from 0 to 447, as said below
- rollout_old: bfloat16 [448, 128, 128], P('expert'), may hold values from -6 to 6
Outputs:
- rollout_new: bfloat16 [448, 128, 128], P('expert')
The draws below stay inside these ranges and needn't reach their ends.
Inputs may be any that keep to these rules, and one draw needn't show every extreme that they name: `held_block`: each of the 224 block numbers stands in exactly one slot, -1 in the others; a trainer device holds at most 1 block. `block_dest`: distinct values; a slot's owner is its value // 28. Some owner receives exactly 28 blocks. The blocks held by the trainer devices of one expert index and destined to one owner number at most 2, and some such pair reaches 2.
All inputs are finite; a program needn't handle non-finite values.
Results may differ from the reference program's by a relative error of at most 0.001.
Values may be sent and summed in bfloat16 or wider, within the bound.
A program may use at most 32 MiB of HBM per device.

```python
import math
import jax
import jax.numpy as jnp

BS = 128
NB = 224
TCAP = 1
CAP = 28
N_FSDP = 64
N_EXPERT = 16
DEVICES = 1024


def layout(key):
    k_busy, k_slot, k_perm, k_off, k_rank, k_row, k_col = jax.random.split(key, 7)
    total_slots = N_EXPERT * CAP
    busiest = jax.random.randint(k_busy, (), 0, N_EXPERT)
    slot_ids = jnp.arange(total_slots, dtype=jnp.int32)
    shuffled = jax.random.permutation(k_slot, total_slots).astype(jnp.int32)
    priority = jnp.where(slot_ids // CAP == busiest, shuffled - total_slots, shuffled)
    slot_order = jnp.argsort(priority, stable=True).astype(jnp.int32)
    block_perm = jax.random.permutation(k_perm, NB).astype(jnp.int32)
    destination = jnp.zeros((NB,), jnp.int32).at[block_perm].set(slot_order[:NB])
    offset = jax.random.randint(k_off, (N_EXPERT,), 0, N_EXPERT).astype(jnp.int32)
    column = (destination % CAP + offset[destination // CAP]) % N_EXPERT
    tiebreak = jax.random.permutation(k_rank, NB).astype(jnp.int32)
    sorted_blocks = jnp.argsort(column * NB + tiebreak, stable=True).astype(jnp.int32)
    counts = jnp.sum((column[:, None] == jnp.arange(N_EXPERT, dtype=jnp.int32)[None, :]).astype(jnp.int32), axis=0)
    starts = jnp.cumsum(counts) - counts
    sorted_col = column[sorted_blocks]
    rank_sorted = jnp.arange(NB, dtype=jnp.int32) - starts[sorted_col]
    col_rank = jnp.zeros((NB,), jnp.int32).at[sorted_blocks].set(rank_sorted.astype(jnp.int32))
    col_width = N_FSDP * TCAP
    full_row = jax.random.randint(k_row, (N_EXPERT,), 0, N_FSDP).astype(jnp.int32)
    cell_ids = jnp.arange(col_width, dtype=jnp.int32)
    scores = jax.random.randint(k_col, (N_EXPERT, col_width), 0, 1 << 16).astype(jnp.int32) * col_width + cell_ids[None, :]
    scores = jnp.where(cell_ids[None, :] // TCAP == full_row[:, None], scores - (1 << 16) * col_width, scores)
    cell_order = jnp.argsort(scores, axis=1, stable=True).astype(jnp.int32)
    cell_index = cell_order[column, col_rank]
    row_index = cell_index // TCAP
    within = cell_index % TCAP
    location = (row_index * N_EXPERT + column) * TCAP + within
    held = jnp.full((DEVICES * TCAP,), -1, jnp.int32).at[location].set(jnp.arange(NB, dtype=jnp.int32))
    return (held, destination)


def draw_held_block(key, part):
    return layout(key)[0]


def draw_block_dest(key, part):
    return layout(key)[1]


def steps_of(key, extent, cuts, least, largest):
    gain, own = 1.0, jax.random.fold_in(key, 6)
    for dim, shards_of in cuts:
        heights = jnp.exp(jax.random.uniform(jax.random.fold_in(own, dim), (shards_of,), jnp.float32, least / len(cuts), largest / len(cuts)))
        gain = gain * jnp.repeat(heights, extent[dim] // shards_of).reshape([-1 if axis == dim else 1 for axis in range(len(extent))])
    return gain


def normal_values(key, extent, spread, reach, cuts=(), kind=jnp.bfloat16):
    result = jax.random.normal(key, extent, jnp.float32) * spread
    if len(cuts) > 0:
        result = steps_of(key, extent, cuts, -0.22, 0.18) * result
    return jnp.clip(result, min=-reach, max=reach).astype(kind)


def setup_inputs(seed: int = 0) -> dict:
    streams_of = jax.random.split(jax.random.key(seed), 6)
    return {
        "deltas": normal_values(streams_of[0], (DEVICES * TCAP, BS, BS), 1.0, 6.0, ((0, 1024),)),
        "scales": jnp.clip(jnp.exp(math.log(0.5) - 2.306499 * jax.random.uniform(streams_of[1], (DEVICES * TCAP,), jnp.float32) ** steps_of(streams_of[1], (DEVICES * TCAP,), ((0, 1024),), -0.2, 0.2)), 0.049804688, 0.5).astype(jnp.bfloat16),
        "held_block": draw_held_block(jax.random.fold_in(streams_of[5], 71), 0),
        "block_dest": draw_block_dest(jax.random.fold_in(streams_of[5], 71), 0),
        "rollout_old": normal_values(streams_of[4], (N_EXPERT * CAP, BS, BS), 1.0, 6.0, ((0, 16),)),
    }


def reference(deltas, scales, held_block, block_dest, rollout_old):
    is_valid = held_block >= 0
    safe_block = jnp.where(is_valid, held_block, 0).astype(jnp.int32)
    slot_index = jnp.where(is_valid, block_dest[safe_block], N_EXPERT * CAP).astype(jnp.int32)
    dequant = deltas.astype(jnp.float32) * scales.astype(jnp.float32)[:, None, None]
    added_sum = jnp.zeros((N_EXPERT * CAP, BS, BS), jnp.float32).at[slot_index].add(dequant, mode="drop")
    return (rollout_old.astype(jnp.float32) + added_sum).astype(jnp.bfloat16)
```

```python
import functools

import jax
import jax.numpy as jnp
from jax import lax
from jax.experimental import pallas as pl
from jax.experimental.pallas import tpu as pltpu
from jax.sharding import PartitionSpec as P

ROWS = 16
LANES = 128
CHUNKS = 8
COLS = 8
OWNERS = 16
PAIR = 2
TILES = CHUNKS * 2 * PAIR
F32 = jnp.float32
BF16 = jnp.bfloat16


def iota(shape, dim):
    return lax.broadcasted_iota(jnp.int32, shape, dim)


def own_meta(f, capacity, scale_ref, held_ref, dest_ref):
    held = held_ref[0]
    dest = dest_ref[jnp.maximum(held, 0)]
    owner = jnp.where(held >= 0, lax.div(dest, capacity) + 1, 0).astype(F32)
    slot = jnp.where(held >= 0, lax.rem(dest, capacity) + 1, 0).astype(F32)
    scale = jnp.broadcast_to(scale_ref[...].astype(F32), (ROWS, LANES))
    row, lane = iota((ROWS, LANES), 0), iota((ROWS, LANES), 1)
    value = jnp.where(row == 0, owner, jnp.where(row == 1, slot, jnp.where(row == 2, scale, 0.0)))
    return jnp.where(lane == f, value, 0.0).astype(BF16)


def select_blocks(e, raw, sendz):
    count = raw.shape[0]
    total = jnp.sum(raw[:, 1].astype(F32), axis=0)
    owner, slot, scale = total[0:1], total[1:2], total[2:3]
    onehot = (iota((OWNERS, LANES), 0).astype(F32) + 1.0 == owner).astype(F32)
    earlier = (iota((LANES, LANES), 0) < iota((LANES, LANES), 1)).astype(F32).astype(BF16)
    before = jnp.dot(onehot.astype(BF16), earlier, preferred_element_type=F32)
    rank = jnp.sum(onehot * before, axis=0, keepdims=True)
    place = jnp.where(owner > 0.0, rank * OWNERS + owner - 1.0, -64.0)
    wide = count * ROWS
    spread = (iota((LANES, wide), 0) == iota((LANES, wide), 1) // ROWS).astype(F32).astype(BF16)
    places = jnp.dot(jnp.broadcast_to(place, (8, LANES)).astype(BF16), spread, preferred_element_type=F32)[0:1]
    target = places.astype(jnp.int32) * ROWS + iota((1, wide), 1) % ROWS
    tall = PAIR * OWNERS * ROWS
    choose = (iota((tall, wide), 0) == target).astype(F32).astype(BF16)
    data = raw[:, 0].reshape(wide, LANES)
    chosen = jnp.dot(choose, data, preferred_element_type=F32).astype(BF16).reshape(PAIR, OWNERS, ROWS, LANES)
    for k in range(PAIR):
        sendz[:, k] = chosen[k]
    mine = iota((PAIR * OWNERS, LANES), 0).astype(F32) == place
    slots = jnp.sum(jnp.where(mine, slot, 0.0), axis=1, keepdims=True)
    scales = jnp.sum(jnp.where(mine, scale, 0.0), axis=1, keepdims=True)
    lane = iota((OWNERS, LANES), 1)
    q, half = lax.rem(e, COLS), lax.div(e, COLS)
    start = lax.rem(q, 2) * 64 + half * 32
    first = (lane >= start) & (lane < start + ROWS)
    second = (lane >= start + ROWS) & (lane < start + 2 * ROWS)

    def placed(column):
        return jnp.where(first, column[:OWNERS], jnp.where(second, column[OWNERS:], 0.0))

    slots, scales = placed(slots), placed(scales)
    row = iota((ROWS, LANES), 0)
    at = 2 * lax.div(q, 2)
    for o in range(OWNERS):
        tile = jnp.where(row == at, slots[o : o + 1], jnp.where(row == at + 1, scales[o : o + 1], 0.0))
        sendz[o, 2] = tile.astype(BF16)


def kernel(
    capacity, scale_ref, held_ref, dest_ref, deltas_ref, old_ref, out_ref,
    sb, raw, sendz, zbuf, grid, old, in_sem, old_sem,
    send1, recv1, send2, recv2, send3, recv3, send4, recv4, send5, recv5,
):
    f, e = lax.axis_index("fsdp"), lax.axis_index("expert")
    r, q = lax.div(f, COLS), lax.rem(f, COLS)
    x, core = lax.div(q, 2), lax.rem(q, 2)
    plane_q, half = lax.rem(e, COLS), lax.div(e, COLS)
    collects = q == plane_q

    def remote(src, dst, send, recv, to_f, to_e):
        return pltpu.make_async_remote_copy(
            src_ref=src, dst_ref=dst, send_sem=send, recv_sem=recv,
            device_id={"fsdp": to_f, "expert": to_e}, device_id_type=pl.DeviceIdType.MESH,
        )

    def wait_bytes(ref, sem):
        pltpu.make_async_copy(ref, ref, sem).wait()

    fetch = pltpu.make_async_copy(deltas_ref, sb.at[:, 0], in_sem)
    fetch.start()
    fetch_old = pltpu.make_async_copy(old_ref, old, old_sem)
    fetch_old.start()
    meta = own_meta(f, capacity, scale_ref, held_ref, dest_ref)
    for chunk in range(CHUNKS):
        sb[chunk, 1] = meta
    fetch.wait()

    for i in range(CHUNKS):
        def send_chunk(i=i):
            remote(sb.at[i], raw.at[f], send1, recv1, i * COLS + plane_q, e).start()
        if_other = jnp.logical_not(collects & (r == i))
        pl.when(if_other)(send_chunk)

    @pl.when(collects)
    def _():
        raw[f] = sb[r]
        wait_bytes(raw.at[pl.ds(0, CHUNKS * COLS - 1)], recv1)
        select_blocks(e, raw, sendz)
        for d in range(1, OWNERS):
            to = lax.rem(e + d, OWNERS)
            remote(sendz.at[to], zbuf.at[half], send2, recv2.at[half], f, to).start()
        zbuf[half] = sendz[e]
        wait_bytes(sb.at[pl.ds(0, CHUNKS - 1)], send1)

    @pl.when(jnp.logical_not(collects))
    def _():
        wait_bytes(sb, send1)

    for h in range(2):
        def arrive(h=h):
            wait_bytes(zbuf.at[h], recv2.at[h])
        pl.when(jnp.logical_not(collects & (half == h)))(arrive)
    for h in range(2):
        for k in range(PAIR):
            grid[q, r * 4 + h * PAIR + k] = zbuf[h, k]
    grid[q, TILES] = zbuf[0, 2] + zbuf[1, 2]

    for d in range(1, CHUNKS):
        to = lax.rem(r + d, CHUNKS)
        part = grid.at[q, pl.ds(r * 4, 4)]
        remote(part, part, send3, recv3, to * COLS + q, e).start()
    wait_bytes(grid.at[q, pl.ds(0, 4 * (CHUNKS - 1))], recv3)

    for d in range(1, 4):
        to = lax.rem(x + d, 4)
        remote(grid.at[q], grid.at[q], send4, recv4.at[d - 1], r * COLS + to * 2 + core, e).start()
    sibling = r * COLS + x * 2 + (1 - core)
    remote(grid.at[q], grid.at[q], send5, recv5.at[0], sibling, e).start()
    for d in range(1, 4):
        src = lax.rem(x + 4 - d, 4) * 2 + core
        wait_bytes(grid.at[src], recv4.at[d - 1])
        remote(grid.at[src], grid.at[src], send5, recv5.at[d], sibling, e).start()
    for d in range(4):
        src = lax.rem(x + 4 - d, 4) * 2 + (1 - core)
        wait_bytes(grid.at[src], recv5.at[d])

    total = jnp.sum(grid[:, TILES].astype(F32), axis=0)
    slots = jnp.concatenate([total[2 * g : 2 * g + 1] for g in range(4)], axis=1)
    scales = jnp.concatenate([total[2 * g + 1 : 2 * g + 2] for g in range(4)], axis=1)
    deep = 4 * LANES
    target = (slots.astype(jnp.int32) - 1) * ROWS + iota((1, deep), 1) % ROWS
    tall = capacity * ROWS
    weights = jnp.where(iota((tall, deep), 0) == target, scales, 0.0).astype(BF16)
    fetch_old.wait()
    for i in range(CHUNKS):
        values = grid[:, pl.ds(i * 4, 4)].reshape(deep, LANES)
        update = jnp.dot(weights, values, preferred_element_type=F32)
        new = old[:, i].astype(F32) + update.reshape(capacity, ROWS, LANES)
        out_ref[:, i] = new.astype(BF16)

    wait_bytes(grid.at[q, pl.ds(0, 4 * (CHUNKS - 1))], send3)
    wait_bytes(grid.at[pl.ds(0, 3)], send4)
    wait_bytes(grid.at[pl.ds(0, 4)], send5)

    @pl.when(collects)
    def _():
        wait_bytes(sendz.at[pl.ds(0, OWNERS - 1)], send2)


def shards(deltas, scales, held_block, block_dest, rollout_old):
    capacity, size = rollout_old.shape[0], rollout_old.shape[1]
    count = CHUNKS * COLS
    dma, vmem = pltpu.SemaphoreType.DMA, pltpu.VMEM
    out = pl.pallas_call(
        functools.partial(kernel, capacity),
        out_shape=jax.ShapeDtypeStruct((capacity, CHUNKS, ROWS, LANES), BF16),
        in_specs=[
            pl.BlockSpec(memory_space=pltpu.VMEM),
            pl.BlockSpec(memory_space=pltpu.SMEM),
            pl.BlockSpec(memory_space=pltpu.SMEM),
            pl.BlockSpec(memory_space=pl.ANY),
            pl.BlockSpec(memory_space=pl.ANY),
        ],
        out_specs=pl.BlockSpec(memory_space=pltpu.VMEM),
        scratch_shapes=[
            vmem((CHUNKS, 2, ROWS, LANES), BF16),
            vmem((count, 2, ROWS, LANES), BF16),
            vmem((OWNERS, 3, ROWS, LANES), BF16),
            vmem((2, 3, ROWS, LANES), BF16),
            vmem((COLS, TILES + 1, ROWS, LANES), BF16),
            vmem((capacity, CHUNKS, ROWS, LANES), BF16),
            dma, dma,
            dma, dma,
            dma, dma((2,)),
            dma, dma,
            dma, dma((3,)),
            dma, dma((4,)),
        ],
        compiler_params=pltpu.CompilerParams(has_side_effects=True, vmem_limit_bytes=48 * 1024 * 1024),
    )(
        scales.reshape(1, 1),
        held_block,
        block_dest,
        deltas.reshape(CHUNKS, ROWS, LANES),
        rollout_old.reshape(capacity, CHUNKS, ROWS, LANES),
    )
    return out.reshape(capacity, size, size)


def solution(mesh):
    in_specs = (
        P(("fsdp", "expert"), None, None),
        P(("fsdp", "expert")),
        P(("fsdp", "expert")),
        P(),
        P("expert", None, None),
    )
    return jax.shard_map(shards, mesh=mesh, in_specs=in_specs, out_specs=P("expert", None, None), check_vma=False)
```

```python
import functools

import jax
import jax.numpy as jnp
from jax import lax
from jax.experimental import pallas as pl
from jax.experimental.pallas import tpu as pltpu
from jax.sharding import PartitionSpec as P

ROWS = 16
LANES = 128
CHUNKS = 8
COLS = 8
OWNERS = 16
PAIR = 2
TILES = CHUNKS * 2 * PAIR
F32 = jnp.float32
BF16 = jnp.bfloat16


def iota(shape, dim):
    return lax.broadcasted_iota(jnp.int32, shape, dim)


def own_meta(f, capacity, scale_ref, held_ref, dest_ref):
    held = held_ref[0]
    dest = dest_ref[jnp.maximum(held, 0)]
    owner = jnp.where(held >= 0, lax.div(dest, capacity) + 1, 0).astype(F32)
    slot = jnp.where(held >= 0, lax.rem(dest, capacity) + 1, 0).astype(F32)
    scale = jnp.broadcast_to(scale_ref[...].astype(F32).reshape(1, 1), (ROWS, LANES))
    row, lane = iota((ROWS, LANES), 0), iota((ROWS, LANES), 1)
    value = jnp.where(row == 0, owner, jnp.where(row == 1, slot, jnp.where(row == 2, scale, 0.0)))
    return jnp.where(lane == f, value, 0.0).astype(BF16)


def select_blocks(e, raw, sendz):
    count = raw.shape[0]
    total = jnp.sum(raw[:, 1].astype(F32), axis=0)
    owner, slot, scale = total[0:1], total[1:2], total[2:3]
    onehot = (iota((OWNERS, LANES), 0).astype(F32) + 1.0 == owner).astype(F32)
    earlier = (iota((LANES, LANES), 0) < iota((LANES, LANES), 1)).astype(F32).astype(BF16)
    before = jnp.dot(onehot.astype(BF16), earlier, preferred_element_type=F32)
    rank = jnp.sum(onehot * before, axis=0, keepdims=True)
    place = jnp.where(owner > 0.0, rank * OWNERS + owner - 1.0, -64.0)
    wide = count * ROWS
    spread = (iota((LANES, wide), 0) == iota((LANES, wide), 1) // ROWS).astype(F32).astype(BF16)
    places = jnp.dot(jnp.broadcast_to(place, (8, LANES)).astype(BF16), spread, preferred_element_type=F32)[0:1]
    target = places.astype(jnp.int32) * ROWS + iota((1, wide), 1) % ROWS
    tall = PAIR * OWNERS * ROWS
    choose = (iota((tall, wide), 0) == target).astype(F32).astype(BF16)
    data = raw[:, 0].reshape(wide, LANES)
    chosen = jnp.dot(choose, data, preferred_element_type=F32).astype(BF16).reshape(PAIR, OWNERS, ROWS, LANES)
    for k in range(PAIR):
        sendz[:, k] = chosen[k]
    mine = iota((PAIR * OWNERS, LANES), 0).astype(F32) == place
    slots = jnp.sum(jnp.where(mine, slot, 0.0), axis=1, keepdims=True)
    scales = jnp.sum(jnp.where(mine, scale, 0.0), axis=1, keepdims=True)
    lane = iota((OWNERS, LANES), 1)
    q, half = lax.rem(e, COLS), lax.div(e, COLS)
    start = lax.rem(q, 2) * 64 + half * 32
    first = (lane >= start) & (lane < start + ROWS)
    second = (lane >= start + ROWS) & (lane < start + 2 * ROWS)

    def placed(column):
        return jnp.where(first, column[:OWNERS], jnp.where(second, column[OWNERS:], 0.0))

    slots, scales = placed(slots), placed(scales)
    row = iota((ROWS, LANES), 0)
    at = 2 * lax.div(q, 2)
    for o in range(OWNERS):
        tile = jnp.where(row == at, slots[o : o + 1], jnp.where(row == at + 1, scales[o : o + 1], 0.0))
        sendz[o, 2] = tile.astype(BF16)


def kernel(
    capacity, scale_hbm, held_hbm, dest_hbm, deltas_ref, old_ref, out_ref,
    scale_ref, held_ref, dest_ref, sb, raw, sendz, zbuf, grid, old, in_sem, old_sem, small_sem,
    send1, recv1, send2, recv2, send3, recv3, send4, recv4, send5, recv5,
):
    f, e = lax.axis_index("fsdp"), lax.axis_index("expert")
    r, q = lax.div(f, COLS), lax.rem(f, COLS)
    x, core = lax.div(q, 2), lax.rem(q, 2)
    plane_q, half = lax.rem(e, COLS), lax.div(e, COLS)
    collects = q == plane_q

    def remote(src, dst, send, recv, to_f, to_e):
        return pltpu.make_async_remote_copy(
            src_ref=src, dst_ref=dst, send_sem=send, recv_sem=recv,
            device_id={"fsdp": to_f, "expert": to_e}, device_id_type=pl.DeviceIdType.MESH,
        )

    def wait_bytes(ref, sem):
        pltpu.make_async_copy(ref, ref, sem).wait()

    fetch = pltpu.make_async_copy(deltas_ref, sb.at[:, 0], in_sem)
    fetch.start()
    fetch_old = pltpu.make_async_copy(old_ref, old, old_sem)
    fetch_old.start()
    small = [
        pltpu.make_async_copy(src, dst, small_sem.at[i])
        for i, (src, dst) in enumerate([(scale_hbm, scale_ref), (held_hbm, held_ref), (dest_hbm, dest_ref)])
    ]
    for copy in small:
        copy.start()

    barrier = pltpu.get_barrier_semaphore()

    def greet(to_f, to_e):
        pl.semaphore_signal(
            barrier, inc=1, device_id={"fsdp": to_f, "expert": to_e}, device_id_type=pl.DeviceIdType.MESH
        )

    @pl.when(collects)
    def _():
        @pl.loop(1, CHUNKS * COLS)
        def _(d):
            greet(lax.rem(f + d, CHUNKS * COLS), e)

    for h in range(2):
        pl.when(e != q + COLS * h)(functools.partial(greet, f, q + COLS * h))
    for d in range(1, CHUNKS):
        greet(lax.rem(r + d, CHUNKS) * COLS + q, e)
    for d in range(1, 4):
        greet(r * COLS + lax.rem(x + d, 4) * 2 + core, e)
    sibling = r * COLS + x * 2 + (1 - core)
    greet(sibling, e)

    for copy in small:
        copy.wait()
    meta = own_meta(f, capacity, scale_ref, held_ref, dest_ref)
    for chunk in range(CHUNKS):
        sb[chunk, 1] = meta
    fetch.wait()

    @pl.when(collects)
    def _():
        pl.semaphore_wait(barrier, 2 * (CHUNKS - 1) + OWNERS - 1 + 4)

    @pl.when(jnp.logical_not(collects))
    def _():
        pl.semaphore_wait(barrier, CHUNKS + CHUNKS - 1 + 4)

    for i in range(CHUNKS):
        def send_chunk(i=i):
            remote(sb.at[i], raw.at[f], send1, recv1, i * COLS + plane_q, e).start()
        if_other = jnp.logical_not(collects & (r == i))
        pl.when(if_other)(send_chunk)

    @pl.when(collects)
    def _():
        raw[f] = sb[r]
        wait_bytes(raw.at[pl.ds(0, CHUNKS * COLS - 1)], recv1)
        select_blocks(e, raw, sendz)
        for d in range(1, OWNERS):
            to = lax.rem(e + d, OWNERS)
            remote(sendz.at[to], zbuf.at[half], send2, recv2.at[half], f, to).start()
        zbuf[half] = sendz[e]
        wait_bytes(sb.at[pl.ds(0, CHUNKS - 1)], send1)

    @pl.when(jnp.logical_not(collects))
    def _():
        wait_bytes(sb, send1)

    for h in range(2):
        def arrive(h=h):
            wait_bytes(zbuf.at[h], recv2.at[h])
        pl.when(jnp.logical_not(collects & (half == h)))(arrive)
    for h in range(2):
        for k in range(PAIR):
            grid[q, r * 4 + h * PAIR + k] = zbuf[h, k]
    grid[q, TILES] = zbuf[0, 2] + zbuf[1, 2]

    for d in range(1, CHUNKS):
        to = lax.rem(r + d, CHUNKS)
        part = grid.at[q, pl.ds(r * 4, 4)]
        remote(part, part, send3, recv3, to * COLS + q, e).start()
    wait_bytes(grid.at[q, pl.ds(0, 4 * (CHUNKS - 1))], recv3)

    for d in range(1, 4):
        to = lax.rem(x + d, 4)
        remote(grid.at[q], grid.at[q], send4, recv4.at[d - 1], r * COLS + to * 2 + core, e).start()
    remote(grid.at[q], grid.at[q], send5, recv5.at[0], sibling, e).start()
    for d in range(1, 4):
        src = lax.rem(x + 4 - d, 4) * 2 + core
        wait_bytes(grid.at[src], recv4.at[d - 1])
        remote(grid.at[src], grid.at[src], send5, recv5.at[d], sibling, e).start()
    for d in range(4):
        src = lax.rem(x + 4 - d, 4) * 2 + (1 - core)
        wait_bytes(grid.at[src], recv5.at[d])

    total = jnp.sum(grid[:, TILES].astype(F32), axis=0)
    slots = jnp.concatenate([total[2 * g : 2 * g + 1] for g in range(4)], axis=1)
    scales = jnp.concatenate([total[2 * g + 1 : 2 * g + 2] for g in range(4)], axis=1)
    deep = 4 * LANES
    target = (slots.astype(jnp.int32) - 1) * ROWS + iota((1, deep), 1) % ROWS
    tall = capacity * ROWS
    weights = jnp.where(iota((tall, deep), 0) == target, scales, 0.0).astype(BF16)
    fetch_old.wait()
    for i in range(CHUNKS):
        values = grid[:, pl.ds(i * 4, 4)].reshape(deep, LANES)
        update = jnp.dot(weights, values, preferred_element_type=F32)
        new = old[:, i].astype(F32) + update.reshape(capacity, ROWS, LANES)
        out_ref[:, i] = new.astype(BF16)

    wait_bytes(grid.at[q, pl.ds(0, 4 * (CHUNKS - 1))], send3)
    wait_bytes(grid.at[pl.ds(0, 3)], send4)
    wait_bytes(grid.at[pl.ds(0, 4)], send5)

    @pl.when(collects)
    def _():
        wait_bytes(sendz.at[pl.ds(0, OWNERS - 1)], send2)


def shards(deltas, scales, held_block, block_dest, rollout_old):
    capacity, size = rollout_old.shape[0], rollout_old.shape[1]
    count = CHUNKS * COLS
    dma, vmem = pltpu.SemaphoreType.DMA, pltpu.VMEM
    out = pl.pallas_call(
        functools.partial(kernel, capacity),
        out_shape=jax.ShapeDtypeStruct((capacity, CHUNKS, ROWS, LANES), BF16),
        in_specs=[
            pl.BlockSpec(memory_space=pltpu.HBM),
            pl.BlockSpec(memory_space=pltpu.HBM),
            pl.BlockSpec(memory_space=pltpu.HBM),
            pl.BlockSpec(memory_space=pltpu.HBM),
            pl.BlockSpec(memory_space=pltpu.HBM),
        ],
        out_specs=pl.BlockSpec(memory_space=pltpu.VMEM),
        scratch_shapes=[
            vmem((1,), BF16), pltpu.SMEM((1,), jnp.int32), pltpu.SMEM(block_dest.shape, jnp.int32),
            vmem((CHUNKS, 2, ROWS, LANES), BF16),
            vmem((count, 2, ROWS, LANES), BF16),
            vmem((OWNERS, 3, ROWS, LANES), BF16),
            vmem((2, 3, ROWS, LANES), BF16),
            vmem((COLS, TILES + 1, ROWS, LANES), BF16),
            vmem((capacity, CHUNKS, ROWS, LANES), BF16),
            dma, dma, dma((3,)),
            dma, dma,
            dma, dma((2,)),
            dma, dma,
            dma, dma((3,)),
            dma, dma((4,)),
        ],
        compiler_params=pltpu.CompilerParams(
            collective_id=1, has_side_effects=True, vmem_limit_bytes=60 * 1024 * 1024
        ),
    )(
        scales,
        held_block,
        block_dest,
        deltas.reshape(CHUNKS, ROWS, LANES),
        rollout_old.reshape(capacity, CHUNKS, ROWS, LANES),
    )
    return out.reshape(capacity, size, size)


def solution(mesh):
    in_specs = (
        P(("fsdp", "expert"), None, None),
        P(("fsdp", "expert")),
        P(("fsdp", "expert")),
        P(),
        P("expert", None, None),
    )
    return jax.shard_map(shards, mesh=mesh, in_specs=in_specs, out_specs=P("expert", None, None), check_vma=False)
```

```python
import functools

import jax
import jax.numpy as jnp
from jax import lax
from jax.experimental import pallas as pl
from jax.experimental.pallas import tpu as pltpu
from jax.sharding import PartitionSpec as P

ROWS = 16
LANES = 128
CHUNKS = 8
COLS = 8
OWNERS = 16
PAIR = 2
TILES = CHUNKS * 2 * PAIR
F32 = jnp.float32
BF16 = jnp.bfloat16


def iota(shape, dim):
    return lax.broadcasted_iota(jnp.int32, shape, dim)


def own_meta(f, capacity, scale_ref, held_ref, dest_ref):
    held = held_ref[0]
    dest = dest_ref[jnp.maximum(held, 0)]
    owner = jnp.where(held >= 0, lax.div(dest, capacity) + 1, 0).astype(F32)
    slot = jnp.where(held >= 0, lax.rem(dest, capacity) + 1, 0).astype(F32)
    scale = jnp.broadcast_to(scale_ref[...].astype(F32).reshape(1, 1), (ROWS, LANES))
    row, lane = iota((ROWS, LANES), 0), iota((ROWS, LANES), 1)
    value = jnp.where(row == 0, owner, jnp.where(row == 1, slot, jnp.where(row == 2, scale, 0.0)))
    return jnp.where(lane == f, value, 0.0).astype(BF16)


def select_blocks(e, raw, sendz):
    count = raw.shape[0]
    total = jnp.sum(raw[:, 1].astype(F32), axis=0)
    owner, slot, scale = total[0:1], total[1:2], total[2:3]
    onehot = (iota((OWNERS, LANES), 0).astype(F32) + 1.0 == owner).astype(F32)
    earlier = (iota((LANES, LANES), 0) < iota((LANES, LANES), 1)).astype(F32).astype(BF16)
    before = jnp.dot(onehot.astype(BF16), earlier, preferred_element_type=F32)
    rank = jnp.sum(onehot * before, axis=0, keepdims=True)
    place = jnp.where(owner > 0.0, rank * OWNERS + owner - 1.0, -64.0)
    wide = count * ROWS
    spread = (iota((LANES, wide), 0) == iota((LANES, wide), 1) // ROWS).astype(F32).astype(BF16)
    places = jnp.dot(jnp.broadcast_to(place, (8, LANES)).astype(BF16), spread, preferred_element_type=F32)[0:1]
    target = places.astype(jnp.int32) * ROWS + iota((1, wide), 1) % ROWS
    tall = PAIR * OWNERS * ROWS
    choose = (iota((tall, wide), 0) == target).astype(F32).astype(BF16)
    data = raw[:, 0].reshape(wide, LANES)
    chosen = jnp.dot(choose, data, preferred_element_type=F32).astype(BF16).reshape(PAIR, OWNERS, ROWS, LANES)
    for k in range(PAIR):
        sendz[:, k] = chosen[k]
    mine = iota((PAIR * OWNERS, LANES), 0).astype(F32) == place
    slots = jnp.sum(jnp.where(mine, slot, 0.0), axis=1, keepdims=True)
    scales = jnp.sum(jnp.where(mine, scale, 0.0), axis=1, keepdims=True)
    lane = iota((OWNERS, LANES), 1)
    q, half = lax.rem(e, COLS), lax.div(e, COLS)
    start = lax.rem(q, 2) * 64 + half * 32
    first = (lane >= start) & (lane < start + ROWS)
    second = (lane >= start + ROWS) & (lane < start + 2 * ROWS)

    def placed(column):
        return jnp.where(first, column[:OWNERS], jnp.where(second, column[OWNERS:], 0.0))

    slots, scales = placed(slots), placed(scales)
    row = iota((ROWS, LANES), 0)
    at = 2 * lax.div(q, 2)
    for o in range(OWNERS):
        tile = jnp.where(row == at, slots[o : o + 1], jnp.where(row == at + 1, scales[o : o + 1], 0.0))
        sendz[o, 2] = tile.astype(BF16)


def kernel(
    capacity, scale_hbm, held_hbm, dest_hbm, deltas_ref, old_ref, out_ref,
    scale_ref, held_ref, dest_ref, sb, raw, sendz, zbuf, grid, old, in_sem, old_sem, small_sem,
    send1, recv1, send2, recv2, send3, recv3, send4, recv4, send5, recv5,
):
    f, e = lax.axis_index("fsdp"), lax.axis_index("expert")
    r, q = lax.div(f, COLS), lax.rem(f, COLS)
    x, core = lax.div(q, 2), lax.rem(q, 2)
    plane_q, half = lax.rem(e, COLS), lax.div(e, COLS)
    collects = q == plane_q

    def remote(src, dst, send, recv, to_f, to_e):
        return pltpu.make_async_remote_copy(
            src_ref=src, dst_ref=dst, send_sem=send, recv_sem=recv,
            device_id={"fsdp": to_f, "expert": to_e}, device_id_type=pl.DeviceIdType.MESH,
        )

    def wait_bytes(ref, sem):
        pltpu.make_async_copy(ref, ref, sem).wait()

    barrier = pltpu.get_barrier_semaphore()

    def greet(to_f, to_e):
        pl.semaphore_signal(
            barrier, inc=1, device_id={"fsdp": to_f, "expert": to_e}, device_id_type=pl.DeviceIdType.MESH
        )

    @pl.when(collects)
    def _():
        for d in range(1, CHUNKS * COLS):
            greet(lax.rem(f + d, CHUNKS * COLS), e)

    for h in range(2):
        pl.when(e != q + COLS * h)(functools.partial(greet, f, q + COLS * h))
    for d in range(1, CHUNKS):
        greet(lax.rem(r + d, CHUNKS) * COLS + q, e)
    for d in range(1, 4):
        greet(r * COLS + lax.rem(x + d, 4) * 2 + core, e)
    sibling = r * COLS + x * 2 + (1 - core)
    greet(sibling, e)

    fetch = pltpu.make_async_copy(deltas_ref, sb.at[:, 0], in_sem)
    fetch.start()
    fetch_old = pltpu.make_async_copy(old_ref, old, old_sem)
    fetch_old.start()
    small = [
        pltpu.make_async_copy(src, dst, small_sem.at[i])
        for i, (src, dst) in enumerate([(scale_hbm, scale_ref), (held_hbm, held_ref), (dest_hbm, dest_ref)])
    ]
    for copy in small:
        copy.start()

    for copy in small:
        copy.wait()
    meta = own_meta(f, capacity, scale_ref, held_ref, dest_ref)
    for chunk in range(CHUNKS):
        sb[chunk, 1] = meta
    fetch.wait()

    @pl.when(collects)
    def _():
        pl.semaphore_wait(barrier, 2 * (CHUNKS - 1) + OWNERS - 1 + 4)

    @pl.when(jnp.logical_not(collects))
    def _():
        pl.semaphore_wait(barrier, CHUNKS + CHUNKS - 1 + 4)

    for i in range(CHUNKS):
        def send_chunk(i=i):
            remote(sb.at[i], raw.at[f], send1, recv1, i * COLS + plane_q, e).start()
        if_other = jnp.logical_not(collects & (r == i))
        pl.when(if_other)(send_chunk)

    @pl.when(collects)
    def _():
        raw[f] = sb[r]
        wait_bytes(raw.at[pl.ds(0, CHUNKS * COLS - 1)], recv1)
        select_blocks(e, raw, sendz)
        for d in range(1, OWNERS):
            to = lax.rem(e + d, OWNERS)
            remote(sendz.at[to], zbuf.at[half], send2, recv2.at[half], f, to).start()
        zbuf[half] = sendz[e]
        wait_bytes(sb.at[pl.ds(0, CHUNKS - 1)], send1)

    @pl.when(jnp.logical_not(collects))
    def _():
        wait_bytes(sb, send1)

    for h in range(2):
        def arrive(h=h):
            wait_bytes(zbuf.at[h], recv2.at[h])
        pl.when(jnp.logical_not(collects & (half == h)))(arrive)
    for h in range(2):
        for k in range(PAIR):
            grid[q, r * 4 + h * PAIR + k] = zbuf[h, k]
    grid[q, TILES] = zbuf[0, 2] + zbuf[1, 2]

    def along_x(first, count):
        part = grid.at[q, pl.ds(first, count)]
        for d in (2, 1, 3):
            remote(part, part, send4, recv4.at[d - 1], r * COLS + lax.rem(x + d, 4) * 2 + core, e).start()

    own = grid.at[q, pl.ds(r * 4, 4)]
    for d in (4, 3, 5, 2, 6, 1, 7):
        remote(own, own, send3, recv3.at[d], lax.rem(r + d, CHUNKS) * COLS + q, e).start()
    along_x(r * 4, 4)
    along_x(TILES, 1)
    for d in (1, 7, 2, 6, 3, 5, 4):
        first = lax.rem(r + CHUNKS - d, CHUNKS) * 4
        wait_bytes(grid.at[q, pl.ds(first, 4)], recv3.at[d])
        along_x(first, 4)
    remote(grid.at[q], grid.at[q], send5, recv5.at[0], sibling, e).start()

    for d in range(1, 4):
        src = lax.rem(x + 4 - d, 4) * 2 + core
        wait_bytes(grid.at[src], recv4.at[d - 1])
        remote(grid.at[src], grid.at[src], send5, recv5.at[d], sibling, e).start()
    for d in range(4):
        src = lax.rem(x + 4 - d, 4) * 2 + (1 - core)
        wait_bytes(grid.at[src], recv5.at[d])

    total = jnp.sum(grid[:, TILES].astype(F32), axis=0)
    slots = jnp.concatenate([total[2 * g : 2 * g + 1] for g in range(4)], axis=1)
    scales = jnp.concatenate([total[2 * g + 1 : 2 * g + 2] for g in range(4)], axis=1)
    deep = 4 * LANES
    target = (slots.astype(jnp.int32) - 1) * ROWS + iota((1, deep), 1) % ROWS
    tall = capacity * ROWS
    weights = jnp.where(iota((tall, deep), 0) == target, scales, 0.0).astype(BF16)
    fetch_old.wait()
    for i in range(CHUNKS):
        values = grid[:, pl.ds(i * 4, 4)].reshape(deep, LANES)
        update = jnp.dot(weights, values, preferred_element_type=F32)
        new = old[:, i].astype(F32) + update.reshape(capacity, ROWS, LANES)
        out_ref[:, i] = new.astype(BF16)

    wait_bytes(grid.at[q, pl.ds(0, 4 * (CHUNKS - 1))], send3)
    wait_bytes(grid.at[pl.ds(0, 3)], send4)
    wait_bytes(grid.at[pl.ds(0, 4)], send5)

    @pl.when(collects)
    def _():
        wait_bytes(sendz.at[pl.ds(0, OWNERS - 1)], send2)


def near(array):
    return pltpu.with_memory_space_constraint(array, pltpu.HBM)


def shards(deltas, scales, held_block, block_dest, rollout_old):
    capacity, size = rollout_old.shape[0], rollout_old.shape[1]
    count = CHUNKS * COLS
    dma, vmem = pltpu.SemaphoreType.DMA, pltpu.VMEM
    out = pl.pallas_call(
        functools.partial(kernel, capacity),
        out_shape=jax.ShapeDtypeStruct((capacity, CHUNKS, ROWS, LANES), BF16),
        in_specs=[
            pl.BlockSpec(memory_space=pltpu.HBM),
            pl.BlockSpec(memory_space=pltpu.HBM),
            pl.BlockSpec(memory_space=pltpu.HBM),
            pl.BlockSpec(memory_space=pltpu.HBM),
            pl.BlockSpec(memory_space=pltpu.HBM),
        ],
        out_specs=pl.BlockSpec(memory_space=pltpu.VMEM),
        scratch_shapes=[
            vmem((1,), BF16), pltpu.SMEM((1,), jnp.int32), pltpu.SMEM(block_dest.shape, jnp.int32),
            vmem((CHUNKS, 2, ROWS, LANES), BF16),
            vmem((count, 2, ROWS, LANES), BF16),
            vmem((OWNERS, 3, ROWS, LANES), BF16),
            vmem((2, 3, ROWS, LANES), BF16),
            vmem((COLS, TILES + 1, ROWS, LANES), BF16),
            vmem((capacity, CHUNKS, ROWS, LANES), BF16),
            dma, dma, dma((3,)),
            dma, dma,
            dma, dma((2,)),
            dma, dma((CHUNKS,)),
            dma, dma((3,)),
            dma, dma((4,)),
        ],
        compiler_params=pltpu.CompilerParams(
            collective_id=1, has_side_effects=True, vmem_limit_bytes=40 * 1024 * 1024
        ),
    )(
        scales,
        held_block,
        near(block_dest),
        near(deltas.reshape(CHUNKS, ROWS, LANES)),
        near(rollout_old.reshape(capacity, CHUNKS, ROWS, LANES)),
    )
    return out.reshape(capacity, size, size)


def solution(mesh):
    in_specs = (
        P(("fsdp", "expert"), None, None),
        P(("fsdp", "expert")),
        P(("fsdp", "expert")),
        P(),
        P("expert", None, None),
    )
    return jax.shard_map(shards, mesh=mesh, in_specs=in_specs, out_specs=P("expert", None, None), check_vma=False)
```

```python
import functools

import jax
import jax.numpy as jnp
from jax import lax
from jax.experimental import pallas as pl
from jax.experimental.pallas import tpu as pltpu
from jax.sharding import PartitionSpec as P

ROWS = 16
LANES = 128
CHUNKS = 8
ALONG_Y = 8
OWNERS = 16
PAIR = 2
PIECE = 2 * PAIR
TILES = ALONG_Y * PIECE
FAR_FIRST = (4, 3, 5, 2, 6, 1, 7)
F32 = jnp.float32
BF16 = jnp.bfloat16


def home(e):
    return lax.rem(lax.div(e, 2) + 4, ALONG_Y)


def iota(shape, dim):
    return lax.broadcasted_iota(jnp.int32, shape, dim)


def own_meta(f, scale_ref, held_ref, dest_ref):
    held = held_ref[0]
    dest = jnp.where(held >= 0, dest_ref[jnp.maximum(held, 0)] + 1, 0).astype(F32)
    scale = jnp.broadcast_to(scale_ref[...].astype(F32).reshape(1, 1), (1, LANES))
    lane = iota((1, LANES), 1)
    return jnp.where(lane == f, dest, jnp.where(lane == f + LANES // 2, scale, 0.0))


def select_blocks(e, capacity, raw, notes, sendz):
    count = raw.shape[0]
    total = jnp.sum(notes[...], axis=0)
    scale = jnp.concatenate([total[:, LANES // 2 :], total[:, : LANES // 2]], axis=1)
    held = (iota((1, LANES), 1) < LANES // 2) & (total > 0.0)
    whole = jnp.floor((total - 0.5) * (1.0 / capacity))
    owner = jnp.where(held, whole + 1.0, 0.0)
    slot = jnp.where(held, total - whole * capacity, 0.0)
    onehot = (iota((OWNERS, LANES), 0).astype(F32) + 1.0 == owner).astype(F32)
    earlier = (iota((LANES, LANES), 0) < iota((LANES, LANES), 1)).astype(F32).astype(BF16)
    before = jnp.dot(onehot.astype(BF16), earlier, preferred_element_type=F32)
    rank = jnp.sum(onehot * before, axis=0, keepdims=True)
    place = jnp.where(owner > 0.0, rank * OWNERS + owner - 1.0, -64.0)
    wide = count * ROWS
    spread = (iota((LANES, wide), 0) == iota((LANES, wide), 1) // ROWS).astype(F32).astype(BF16)
    places = jnp.dot(jnp.broadcast_to(place, (8, LANES)).astype(BF16), spread, preferred_element_type=F32)[0:1]
    target = places.astype(jnp.int32) * ROWS + iota((1, wide), 1) % ROWS
    tall = PAIR * OWNERS * ROWS
    choose = (iota((tall, wide), 0) == target).astype(F32).astype(BF16)
    data = raw[...].reshape(wide, LANES)
    chosen = jnp.dot(choose, data, preferred_element_type=F32).astype(BF16).reshape(PAIR, OWNERS, ROWS, LANES)
    for k in range(PAIR):
        sendz[:, k] = chosen[k]
    mine = iota((PAIR * OWNERS, LANES), 0).astype(F32) == place
    slots = jnp.sum(jnp.where(mine, slot, 0.0), axis=1, keepdims=True)
    scales = jnp.sum(jnp.where(mine, scale, 0.0), axis=1, keepdims=True)
    lane = iota((OWNERS, LANES), 1)
    q, half = home(e), lax.rem(e, 2)
    start = lax.rem(q, 2) * 64 + half * 32
    first = (lane >= start) & (lane < start + ROWS)
    second = (lane >= start + ROWS) & (lane < start + 2 * ROWS)

    def placed(column):
        return jnp.where(first, column[:OWNERS], jnp.where(second, column[OWNERS:], 0.0))

    slots, scales = placed(slots), placed(scales)
    row = iota((ROWS, LANES), 0)
    at = 2 * lax.div(q, 2)
    for o in range(OWNERS):
        tile = jnp.where(row == at, slots[o : o + 1], jnp.where(row == at + 1, scales[o : o + 1], 0.0))
        sendz[o, 2] = tile.astype(BF16)


def kernel(
    capacity, scale_hbm, held_hbm, dest_hbm, deltas_ref, old_ref, out_ref,
    scale_ref, held_ref, dest_ref, sb, note, raw, notes, sendz, grid, metas, weights, old, in_sem, old_sem, small_sem,
    send1, recv1, send2, recv2, send3, recv3, send4, recv4, send5, recv5, send6, recv6, send7, recv7, send8, recv8, ready,
):
    f, e = lax.axis_index("fsdp"), lax.axis_index("expert")
    y, r = lax.div(f, CHUNKS), lax.rem(f, CHUNKS)
    x, core = lax.div(r, 2), lax.rem(r, 2)
    half = lax.rem(e, 2)
    collects = y == home(e)
    base = lax.rem(y + 4, ALONG_Y) * 2
    count = CHUNKS * ALONG_Y

    def where(to_f, to_e):
        return dict(device_id={"fsdp": to_f, "expert": to_e}, device_id_type=pl.DeviceIdType.MESH)

    def remote(src, dst, send, recv, to_f, to_e):
        return pltpu.make_async_remote_copy(
            src_ref=src, dst_ref=dst, send_sem=send, recv_sem=recv, **where(to_f, to_e)
        )

    def wait_bytes(ref, sem):
        pltpu.make_async_copy(ref, ref, sem).wait()

    barrier = pltpu.get_barrier_semaphore()

    def greet(to_f, to_e):
        pl.semaphore_signal(barrier, inc=1, **where(to_f, to_e))

    @pl.when(collects)
    def _():
        for d in range(1, count):
            greet(lax.rem(f + d, count), e)
        for plane in range(1, OWNERS):
            pl.when(plane > e)(functools.partial(greet, f, plane))

    for h in range(2):
        pl.when(e < base + h)(functools.partial(greet, f, base + h))
    for d in range(1, ALONG_Y):
        greet(lax.rem(f + d * CHUNKS, count), e)
    for d in range(1, 4):
        greet(y * CHUNKS + lax.rem(r + 2 * d, CHUNKS), e)
    sibling = y * CHUNKS + x * 2 + (1 - core)
    greet(sibling, e)

    fetch = pltpu.make_async_copy(deltas_ref, sb, in_sem)
    fetch.start()
    fetch_old = pltpu.make_async_copy(old_ref, old, old_sem)
    fetch_old.start()
    small = [
        pltpu.make_async_copy(src, dst, small_sem.at[i])
        for i, (src, dst) in enumerate([(scale_hbm, scale_ref), (held_hbm, held_ref), (dest_hbm, dest_ref)])
    ]
    for copy in small:
        copy.start()
    for copy in small:
        copy.wait()
    note[...] = own_meta(f, scale_ref, held_ref, dest_ref)
    fetch.wait()

    lower = (base < e).astype(jnp.int32) + (base + 1 < e).astype(jnp.int32)
    pl.semaphore_wait(barrier, ALONG_Y + 3 + lower + jnp.where(collects, CHUNKS - 1 + e, CHUNKS))
    for h in range(2):
        def answer(h=h):
            pl.semaphore_signal(ready, inc=1, **where(f, base + h))
        pl.when(base + h < e)(answer)

    for i in range(CHUNKS):
        def send_chunk(i=i):
            remote(sb.at[i], raw.at[f], send1, recv1, home(e) * CHUNKS + i, e).start()
            remote(note, notes.at[f], send8, recv8, home(e) * CHUNKS + i, e).start()
        pl.when(jnp.logical_not(collects & (r == i)))(send_chunk)

    @pl.when(collects)
    def _():
        raw[f] = sb[r]
        notes[f] = note[...]
        wait_bytes(raw.at[pl.ds(0, count - 1)], recv1)
        wait_bytes(notes.at[pl.ds(0, count - 1)], recv8)
        select_blocks(e, capacity, raw, notes, sendz)
        mine = pl.ds(y * PIECE + half * PAIR, PAIR)
        place = y * 2 + half

        def along_z(plane):
            remote(sendz.at[plane, pl.ds(0, PAIR)], grid.at[r, mine], send2, recv2.at[half], f, plane).start()
            remote(sendz.at[plane, PAIR], metas.at[place], send3, recv3.at[half], f, plane).start()

        for plane in range(OWNERS - 1):
            pl.when(plane < e)(functools.partial(along_z, plane))
        grid[r, mine] = sendz[e, pl.ds(0, PAIR)]
        metas[place] = sendz[e, PAIR]
        pl.when(e < OWNERS - 1)(lambda: pl.semaphore_wait(ready, OWNERS - 1 - e))
        for plane in range(1, OWNERS):
            pl.when(plane > e)(functools.partial(along_z, plane))

    def along_x(row):
        part = grid.at[r, pl.ds(row * PIECE, PIECE)]
        for d in (2, 1, 3):
            remote(part, part, send5, recv5.at[d - 1], y * CHUNKS + lax.rem(r + 2 * d, CHUNKS), e).start()

    def own_piece():
        for h in range(2):
            def arrive(h=h):
                wait_bytes(grid.at[r, pl.ds(y * PIECE + h * PAIR, PAIR)], recv2.at[h])
                wait_bytes(metas.at[y * 2 + h], recv3.at[h])
            pl.when(jnp.logical_not(collects & (half == h)))(arrive)
        part, both = grid.at[r, pl.ds(y * PIECE, PIECE)], metas.at[pl.ds(y * 2, 2)]
        for d in FAR_FIRST:
            remote(part, part, send4, recv4.at[y], lax.rem(f + d * CHUNKS, count), e).start()
        along_x(y)
        for d in FAR_FIRST:
            remote(both, both, send7, recv7, lax.rem(f + d * CHUNKS, count), e).start()

    def other_piece(row):
        def arrive():
            wait_bytes(grid.at[r, pl.ds(row * PIECE, PIECE)], recv4.at[row])
            along_x(row)
        pl.when(y != row)(arrive)

    pl.when(y >= 4)(own_piece)
    for row in range(4, 8):
        other_piece(row)
    pl.when(y < 4)(own_piece)
    for row in range(4):
        other_piece(row)

    remote(grid.at[r], grid.at[r], send6, recv6.at[0], sibling, e).start()
    wait_bytes(metas.at[pl.ds(0, 2 * (ALONG_Y - 1))], recv7)
    total = jnp.sum(metas[...].astype(F32), axis=0)
    slots = jnp.concatenate([total[2 * g : 2 * g + 1] for g in range(4)], axis=1)
    scales = jnp.concatenate([total[2 * g + 1 : 2 * g + 2] for g in range(4)], axis=1)
    deep = 4 * LANES
    target = (slots.astype(jnp.int32) - 1) * ROWS + iota((1, deep), 1) % ROWS
    tall = capacity * ROWS
    weights[...] = jnp.where(iota((tall, deep), 0) == target, scales, 0.0).astype(BF16)
    fetch_old.wait()

    def add(i):
        values = grid[i].reshape(deep, LANES)
        update = jnp.dot(weights[...], values, preferred_element_type=F32)
        new = old[:, i].astype(F32) + update.reshape(capacity, ROWS, LANES)
        out_ref[:, i] = new.astype(BF16)

    for d in (1, 3, 2):
        src = lax.rem(r + CHUNKS - 2 * d, CHUNKS)
        wait_bytes(grid.at[src], recv5.at[d - 1])
        remote(grid.at[src], grid.at[src], send6, recv6.at[d], sibling, e).start()
    for d in range(4):
        add(lax.rem(r + CHUNKS - 2 * d, CHUNKS))
    for d in (0, 1, 3, 2):
        src = lax.rem(r + CHUNKS - 2 * d, CHUNKS) + 1 - 2 * core
        wait_bytes(grid.at[src], recv6.at[d])
        add(src)

    wait_bytes(grid.at[r, pl.ds(0, PIECE * (ALONG_Y - 1))], send4)
    wait_bytes(metas.at[pl.ds(0, 2 * (ALONG_Y - 1))], send7)
    wait_bytes(grid.at[pl.ds(0, 3)], send5)
    wait_bytes(grid.at[pl.ds(0, 4)], send6)

    @pl.when(collects)
    def _():
        wait_bytes(grid.at[r, pl.ds(0, PAIR * (OWNERS - 1))], send2)
        wait_bytes(metas.at[pl.ds(0, OWNERS - 1)], send3)
        wait_bytes(sb.at[pl.ds(0, CHUNKS - 1)], send1)
        wait_bytes(notes.at[pl.ds(0, CHUNKS - 1)], send8)

    @pl.when(jnp.logical_not(collects))
    def _():
        wait_bytes(sb, send1)
        wait_bytes(notes.at[pl.ds(0, CHUNKS)], send8)


def near(array):
    return pltpu.with_memory_space_constraint(array, pltpu.HBM)


def shards(deltas, scales, held_block, block_dest, rollout_old):
    capacity, size = rollout_old.shape[0], rollout_old.shape[1]
    count = CHUNKS * ALONG_Y
    dma, vmem = pltpu.SemaphoreType.DMA, pltpu.VMEM
    out = pl.pallas_call(
        functools.partial(kernel, capacity),
        out_shape=jax.ShapeDtypeStruct((capacity, CHUNKS, ROWS, LANES), BF16),
        in_specs=[
            pl.BlockSpec(memory_space=pltpu.HBM),
            pl.BlockSpec(memory_space=pltpu.HBM),
            pl.BlockSpec(memory_space=pltpu.HBM),
            pl.BlockSpec(memory_space=pltpu.HBM),
            pl.BlockSpec(memory_space=pltpu.HBM),
        ],
        out_specs=pl.BlockSpec(memory_space=pltpu.VMEM),
        scratch_shapes=[
            vmem((1,), BF16), pltpu.SMEM((1,), jnp.int32), pltpu.SMEM(block_dest.shape, jnp.int32),
            vmem((CHUNKS, ROWS, LANES), BF16),
            vmem((1, LANES), F32),
            vmem((count, ROWS, LANES), BF16),
            vmem((count, 1, LANES), F32),
            vmem((OWNERS, PAIR + 1, ROWS, LANES), BF16),
            vmem((CHUNKS, TILES, ROWS, LANES), BF16),
            vmem((OWNERS, ROWS, LANES), BF16),
            vmem((capacity * ROWS, 4 * LANES), BF16),
            vmem((capacity, CHUNKS, ROWS, LANES), BF16),
            dma, dma, dma((3,)),
            dma, dma,
            dma, dma((2,)),
            dma, dma((2,)),
            dma, dma((ALONG_Y,)),
            dma, dma((3,)),
            dma, dma((4,)),
            dma, dma,
            dma, dma,
            pltpu.SemaphoreType.REGULAR,
        ],
        compiler_params=pltpu.CompilerParams(
            collective_id=1, has_side_effects=True, vmem_limit_bytes=40 * 1024 * 1024
        ),
    )(
        scales,
        held_block,
        near(block_dest),
        near(deltas.reshape(CHUNKS, ROWS, LANES)),
        near(rollout_old.reshape(capacity, CHUNKS, ROWS, LANES)),
    )
    return out.reshape(capacity, size, size)


def solution(mesh):
    in_specs = (
        P(("fsdp", "expert"), None, None),
        P(("fsdp", "expert")),
        P(("fsdp", "expert")),
        P(),
        P("expert", None, None),
    )
    return jax.shard_map(shards, mesh=mesh, in_specs=in_specs, out_specs=P("expert", None, None), check_vma=False)
```

```python
import functools

import jax
import jax.numpy as jnp
from jax import lax
from jax.experimental import pallas as pl
from jax.experimental.pallas import tpu as pltpu
from jax.sharding import PartitionSpec as P

ROWS = 16
LANES = 128
CHUNKS = 8
ALONG_Y = 8
OWNERS = 16
PAIR = 2
PIECE = 2 * PAIR
TILES = ALONG_Y * PIECE
FAR_FIRST = (4, 3, 5, 2, 6, 1, 7)
F32 = jnp.float32
BF16 = jnp.bfloat16


def home(e):
    return lax.rem(lax.div(e, 2) + 4, ALONG_Y)


def iota(shape, dim):
    return lax.broadcasted_iota(jnp.int32, shape, dim)


def own_meta(f, scale_ref, held_ref, dest_ref):
    held = held_ref[0]
    dest = jnp.where(held >= 0, dest_ref[jnp.maximum(held, 0)] + 1, 0).astype(F32)
    scale = jnp.broadcast_to(scale_ref[...].astype(F32).reshape(1, 1), (1, LANES))
    lane = iota((1, LANES), 1)
    return jnp.where(lane == f, dest, jnp.where(lane == f + LANES // 2, scale, 0.0))


def plan_blocks(e, capacity, notes, choose, sendz):
    count = notes.shape[0]
    total = jnp.sum(notes[...], axis=0)
    scale = jnp.concatenate([total[:, LANES // 2 :], total[:, : LANES // 2]], axis=1)
    held = (iota((1, LANES), 1) < LANES // 2) & (total > 0.0)
    whole = jnp.floor((total - 0.5) * (1.0 / capacity))
    owner = jnp.where(held, whole + 1.0, 0.0)
    slot = jnp.where(held, total - whole * capacity, 0.0)
    onehot = (iota((OWNERS, LANES), 0).astype(F32) + 1.0 == owner).astype(F32)
    earlier = (iota((LANES, LANES), 0) < iota((LANES, LANES), 1)).astype(F32).astype(BF16)
    before = jnp.dot(onehot.astype(BF16), earlier, preferred_element_type=F32)
    rank = jnp.sum(onehot * before, axis=0, keepdims=True)
    place = jnp.where(owner > 0.0, rank * OWNERS + owner - 1.0, -64.0)
    wide = count * ROWS
    spread = (iota((LANES, wide), 0) == iota((LANES, wide), 1) // ROWS).astype(F32).astype(BF16)
    places = jnp.dot(jnp.broadcast_to(place, (8, LANES)).astype(BF16), spread, preferred_element_type=F32)[0:1]
    target = places.astype(jnp.int32) * ROWS + iota((1, wide), 1) % ROWS
    tall = PAIR * OWNERS * ROWS
    choose[...] = (iota((tall, wide), 0) == target).astype(F32).astype(BF16)
    mine = iota((PAIR * OWNERS, LANES), 0).astype(F32) == place
    slots = jnp.sum(jnp.where(mine, slot, 0.0), axis=1, keepdims=True)
    scales = jnp.sum(jnp.where(mine, scale, 0.0), axis=1, keepdims=True)
    lane = iota((OWNERS, LANES), 1)
    q, half = home(e), lax.rem(e, 2)
    start = lax.rem(q, 2) * 64 + half * 32
    first = (lane >= start) & (lane < start + ROWS)
    second = (lane >= start + ROWS) & (lane < start + 2 * ROWS)

    def placed(column):
        return jnp.where(first, column[:OWNERS], jnp.where(second, column[OWNERS:], 0.0))

    slots, scales = placed(slots), placed(scales)
    row = iota((ROWS, LANES), 0)
    at = 2 * lax.div(q, 2)
    for o in range(OWNERS):
        tile = jnp.where(row == at, slots[o : o + 1], jnp.where(row == at + 1, scales[o : o + 1], 0.0))
        sendz[o, 2] = tile.astype(BF16)


def move_blocks(choose, raw, sendz):
    count = raw.shape[0]
    data = raw[...].reshape(count * ROWS, LANES)
    chosen = jnp.dot(choose[...], data, preferred_element_type=F32).astype(BF16).reshape(PAIR, OWNERS, ROWS, LANES)
    for k in range(PAIR):
        sendz[:, k] = chosen[k]


def kernel(
    capacity, scale_hbm, held_hbm, dest_hbm, deltas_ref, old_ref, out_ref,
    scale_ref, held_ref, dest_ref, note, raw, notes, choose, sendz, grid, metas, weights, old, in_sem, old_sem, small_sem,
    send1, recv1, send2, recv2, send3, recv3, send4, recv4, send5, recv5, send6, recv6, send7, recv7, send8, recv8, ready, go,
):
    f, e = lax.axis_index("fsdp"), lax.axis_index("expert")
    y, r = lax.div(f, CHUNKS), lax.rem(f, CHUNKS)
    x, core = lax.div(r, 2), lax.rem(r, 2)
    half = lax.rem(e, 2)
    collects = y == home(e)
    base = lax.rem(y + 4, ALONG_Y) * 2
    count = CHUNKS * ALONG_Y

    def where(to_f, to_e):
        return dict(device_id={"fsdp": to_f, "expert": to_e}, device_id_type=pl.DeviceIdType.MESH)

    def remote(src, dst, send, recv, to_f, to_e):
        return pltpu.make_async_remote_copy(
            src_ref=src, dst_ref=dst, send_sem=send, recv_sem=recv, **where(to_f, to_e)
        )

    def wait_bytes(ref, sem):
        pltpu.make_async_copy(ref, ref, sem).wait()

    small = [
        pltpu.make_async_copy(src, dst, small_sem.at[i])
        for i, (src, dst) in enumerate([(scale_hbm, scale_ref), (held_hbm, held_ref), (dest_hbm, dest_ref)])
    ]
    for copy in small:
        copy.start()

    barrier = pltpu.get_barrier_semaphore()

    def greet(to_f, to_e):
        pl.semaphore_signal(barrier, inc=1, **where(to_f, to_e))

    @pl.when(collects)
    def _():
        for d in FAR_FIRST + (0,):
            for shift in range(d == 0, CHUNKS):
                greet(lax.rem(y + d, ALONG_Y) * CHUNKS + lax.rem(r + shift, CHUNKS), e)
        for plane in range(1, OWNERS):
            pl.when(plane > e)(functools.partial(greet, f, plane))

    sibling = y * CHUNKS + x * 2 + (1 - core)

    for h in range(2):
        pl.when(e < base + h)(functools.partial(greet, f, base + h))

    for copy in small:
        copy.wait()
    note[...] = own_meta(f, scale_ref, held_ref, dest_ref)

    lower = (base < e).astype(jnp.int32) + (base + 1 < e).astype(jnp.int32)
    pl.semaphore_wait(barrier, lower + jnp.where(collects, CHUNKS - 1 + e, CHUNKS))
    for h in range(2):
        def answer(h=h):
            pl.semaphore_signal(ready, inc=1, **where(f, base + h))
        pl.when(base + h < e)(answer)

    for i in range(CHUNKS):
        def send_note(i=i):
            remote(note, notes.at[f], send8, recv8, home(e) * CHUNKS + i, e).start()
        pl.when(jnp.logical_not(collects & (r == i)))(send_note)
    for i in range(CHUNKS):
        def send_chunk(i=i):
            remote(deltas_ref.at[i], raw.at[f], send1, recv1, home(e) * CHUNKS + i, e).start()
        pl.when(jnp.logical_not(collects & (r == i)))(send_chunk)
    fetch_old = pltpu.make_async_copy(old_ref, old, old_sem)
    fetch_old.start()

    @pl.when(collects)
    def _():
        own_chunk = pltpu.make_async_copy(deltas_ref.at[r], raw.at[f], in_sem)
        own_chunk.start()
        notes[f] = note[...]
        own_chunk.wait()
        wait_bytes(notes.at[pl.ds(0, count - 1)], recv8)
        plan_blocks(e, capacity, notes, choose, sendz)
        wait_bytes(raw.at[pl.ds(0, count - 1)], recv1)
        move_blocks(choose, raw, sendz)
        mine = pl.ds(y * PIECE + half * PAIR, PAIR)
        place = y * 2 + half

        def along_z(plane):
            remote(sendz.at[plane, pl.ds(0, PAIR)], grid.at[r, mine], send2, recv2.at[half], f, plane).start()
            remote(sendz.at[plane, PAIR], metas.at[place], send3, recv3.at[half], f, plane).start()

        for plane in range(OWNERS - 1):
            pl.when(plane < e)(functools.partial(along_z, plane))
        grid[r, mine] = sendz[e, pl.ds(0, PAIR)]
        metas[place] = sendz[e, PAIR]
        for d in FAR_FIRST:
            pl.semaphore_signal(go, inc=1, **where(lax.rem(f + d * CHUNKS, count), e))
        pl.when(e < OWNERS - 1)(lambda: pl.semaphore_wait(ready, OWNERS - 1 - e))
        for plane in range(1, OWNERS):
            pl.when(plane > e)(functools.partial(along_z, plane))

    pl.when(jnp.logical_not(collects))(lambda: pl.semaphore_wait(go, 1))

    def along_x(row):
        part = grid.at[r, pl.ds(row * PIECE, PIECE)]
        for d in (2, 1, 3):
            remote(part, part, send5, recv5.at[d - 1], y * CHUNKS + lax.rem(r + 2 * d, CHUNKS), e).start()

    def own_piece():
        for h in range(2):
            def arrive(h=h):
                wait_bytes(grid.at[r, pl.ds(y * PIECE + h * PAIR, PAIR)], recv2.at[h])
                wait_bytes(metas.at[y * 2 + h], recv3.at[h])
            pl.when(jnp.logical_not(collects & (half == h)))(arrive)
        part, both = grid.at[r, pl.ds(y * PIECE, PIECE)], metas.at[pl.ds(y * 2, 2)]
        for d in FAR_FIRST:
            remote(part, part, send4, recv4.at[y], lax.rem(f + d * CHUNKS, count), e).start()
        along_x(y)
        for d in FAR_FIRST:
            remote(both, both, send7, recv7, lax.rem(f + d * CHUNKS, count), e).start()

    def other_piece(row):
        def arrive():
            wait_bytes(grid.at[r, pl.ds(row * PIECE, PIECE)], recv4.at[row])
            along_x(row)
        pl.when(y != row)(arrive)

    pl.when(y >= 4)(own_piece)
    for row in range(4, 8):
        other_piece(row)
    pl.when(y < 4)(own_piece)
    for row in range(4):
        other_piece(row)

    remote(grid.at[r], grid.at[r], send6, recv6.at[0], sibling, e).start()
    wait_bytes(metas.at[pl.ds(0, 2 * (ALONG_Y - 1))], recv7)
    total = jnp.sum(metas[...].astype(F32), axis=0)
    slots = jnp.concatenate([total[2 * g : 2 * g + 1] for g in range(4)], axis=1)
    scales = jnp.concatenate([total[2 * g + 1 : 2 * g + 2] for g in range(4)], axis=1)
    deep = 4 * LANES
    target = (slots.astype(jnp.int32) - 1) * ROWS + iota((1, deep), 1) % ROWS
    tall = capacity * ROWS
    weights[...] = jnp.where(iota((tall, deep), 0) == target, scales, 0.0).astype(BF16)
    fetch_old.wait()

    def add(i):
        values = grid[i].reshape(deep, LANES)
        update = jnp.dot(weights[...], values, preferred_element_type=F32)
        new = old[:, i].astype(F32) + update.reshape(capacity, ROWS, LANES)
        out_ref[:, i] = new.astype(BF16)

    for d in (1, 3, 2):
        src = lax.rem(r + CHUNKS - 2 * d, CHUNKS)
        wait_bytes(grid.at[src], recv5.at[d - 1])
        remote(grid.at[src], grid.at[src], send6, recv6.at[d], sibling, e).start()
    for d in range(4):
        add(lax.rem(r + CHUNKS - 2 * d, CHUNKS))
    for d in (0, 1, 3, 2):
        src = lax.rem(r + CHUNKS - 2 * d, CHUNKS) + 1 - 2 * core
        wait_bytes(grid.at[src], recv6.at[d])
        add(src)

    wait_bytes(grid.at[r, pl.ds(0, PIECE * (ALONG_Y - 1))], send4)
    wait_bytes(metas.at[pl.ds(0, 2 * (ALONG_Y - 1))], send7)
    wait_bytes(grid.at[pl.ds(0, 3)], send5)
    wait_bytes(grid.at[pl.ds(0, 4)], send6)

    @pl.when(collects)
    def _():
        wait_bytes(grid.at[r, pl.ds(0, PAIR * (OWNERS - 1))], send2)
        wait_bytes(metas.at[pl.ds(0, OWNERS - 1)], send3)
        wait_bytes(raw.at[pl.ds(0, CHUNKS - 1)], send1)
        wait_bytes(notes.at[pl.ds(0, CHUNKS - 1)], send8)

    @pl.when(jnp.logical_not(collects))
    def _():
        wait_bytes(raw.at[pl.ds(0, CHUNKS)], send1)
        wait_bytes(notes.at[pl.ds(0, CHUNKS)], send8)


def near(array):
    return pltpu.with_memory_space_constraint(array, pltpu.HBM)


def shards(deltas, scales, held_block, block_dest, rollout_old):
    capacity, size = rollout_old.shape[0], rollout_old.shape[1]
    count = CHUNKS * ALONG_Y
    dma, vmem = pltpu.SemaphoreType.DMA, pltpu.VMEM
    out = pl.pallas_call(
        functools.partial(kernel, capacity),
        out_shape=jax.ShapeDtypeStruct((capacity, CHUNKS, ROWS, LANES), BF16),
        in_specs=[
            pl.BlockSpec(memory_space=pltpu.HBM),
            pl.BlockSpec(memory_space=pltpu.HBM),
            pl.BlockSpec(memory_space=pltpu.HBM),
            pl.BlockSpec(memory_space=pltpu.HBM),
            pl.BlockSpec(memory_space=pltpu.HBM),
        ],
        out_specs=pl.BlockSpec(memory_space=pltpu.VMEM),
        scratch_shapes=[
            vmem((1,), BF16), pltpu.SMEM((1,), jnp.int32), pltpu.SMEM(block_dest.shape, jnp.int32),
            vmem((1, LANES), F32),
            vmem((count, ROWS, LANES), BF16),
            vmem((count, 1, LANES), F32),
            vmem((PAIR * OWNERS * ROWS, count * ROWS), BF16),
            vmem((OWNERS, PAIR + 1, ROWS, LANES), BF16),
            vmem((CHUNKS, TILES, ROWS, LANES), BF16),
            vmem((OWNERS, ROWS, LANES), BF16),
            vmem((capacity * ROWS, 4 * LANES), BF16),
            vmem((capacity, CHUNKS, ROWS, LANES), BF16),
            dma, dma, dma((3,)),
            dma, dma,
            dma, dma((2,)),
            dma, dma((2,)),
            dma, dma((ALONG_Y,)),
            dma, dma((3,)),
            dma, dma((4,)),
            dma, dma,
            dma, dma,
            pltpu.SemaphoreType.REGULAR,
            pltpu.SemaphoreType.REGULAR,
        ],
        compiler_params=pltpu.CompilerParams(
            collective_id=1, has_side_effects=True, vmem_limit_bytes=40 * 1024 * 1024
        ),
    )(
        scales,
        held_block,
        near(block_dest),
        near(deltas.reshape(CHUNKS, ROWS, LANES)),
        near(rollout_old.reshape(capacity, CHUNKS, ROWS, LANES)),
    )
    return out.reshape(capacity, size, size)


def solution(mesh):
    in_specs = (
        P(("fsdp", "expert"), None, None),
        P(("fsdp", "expert")),
        P(("fsdp", "expert")),
        P(),
        P("expert", None, None),
    )
    return jax.shard_map(shards, mesh=mesh, in_specs=in_specs, out_specs=P("expert", None, None), check_vma=False)
```

```python
import functools

import jax
import jax.numpy as jnp
from jax import lax
from jax.experimental import pallas as pl
from jax.experimental.pallas import tpu as pltpu
from jax.sharding import PartitionSpec as P

ROWS = 16
LANES = 128
CHUNKS = 8
ALONG_Y = 8
OWNERS = 16
PAIR = 2
PIECE = 2 * PAIR
TILES = ALONG_Y * PIECE
FAR_FIRST = (4, 3, 5, 2, 6, 1, 7)
F32 = jnp.float32
BF16 = jnp.bfloat16


def home(e):
    return lax.rem(lax.div(e, 2) + 4, ALONG_Y)


def iota(shape, dim):
    return lax.broadcasted_iota(jnp.int32, shape, dim)


def own_meta(f, scale_ref, held_ref, dest_ref):
    held = held_ref[0]
    dest = jnp.where(held >= 0, dest_ref[jnp.maximum(held, 0)] + 1, 0).astype(F32)
    scale = jnp.broadcast_to(scale_ref[...].astype(F32).reshape(1, 1), (1, LANES))
    lane = iota((1, LANES), 1)
    return jnp.where(lane == f, dest, jnp.where(lane == f + LANES // 2, scale, 0.0))


def plan_blocks(e, capacity, notes, choose, sendz):
    count = notes.shape[0]
    total = jnp.sum(notes[...], axis=0)
    scale = jnp.concatenate([total[:, LANES // 2 :], total[:, : LANES // 2]], axis=1)
    held = (iota((1, LANES), 1) < LANES // 2) & (total > 0.0)
    whole = jnp.floor((total - 0.5) * (1.0 / capacity))
    owner = jnp.where(held, whole + 1.0, 0.0)
    slot = jnp.where(held, total - whole * capacity, 0.0)
    onehot = (iota((OWNERS, LANES), 0).astype(F32) + 1.0 == owner).astype(F32)
    earlier = (iota((LANES, LANES), 0) < iota((LANES, LANES), 1)).astype(F32).astype(BF16)
    before = jnp.dot(onehot.astype(BF16), earlier, preferred_element_type=F32)
    rank = jnp.sum(onehot * before, axis=0, keepdims=True)
    place = jnp.where(owner > 0.0, rank * OWNERS + owner - 1.0, -64.0)
    wide = count * ROWS
    spread = (iota((LANES, wide), 0) == iota((LANES, wide), 1) // ROWS).astype(F32).astype(BF16)
    places = jnp.dot(jnp.broadcast_to(place, (8, LANES)).astype(BF16), spread, preferred_element_type=F32)[0:1]
    target = places.astype(jnp.int32) * ROWS + iota((1, wide), 1) % ROWS
    tall = PAIR * OWNERS * ROWS
    choose[...] = (iota((tall, wide), 0) == target).astype(F32).astype(BF16)
    mine = iota((PAIR * OWNERS, LANES), 0).astype(F32) == place
    slots = jnp.sum(jnp.where(mine, slot, 0.0), axis=1, keepdims=True)
    scales = jnp.sum(jnp.where(mine, scale, 0.0), axis=1, keepdims=True)
    lane = iota((OWNERS, LANES), 1)
    q, half = home(e), lax.rem(e, 2)
    start = lax.rem(q, 2) * 64 + half * 32
    first = (lane >= start) & (lane < start + ROWS)
    second = (lane >= start + ROWS) & (lane < start + 2 * ROWS)

    def placed(column):
        return jnp.where(first, column[:OWNERS], jnp.where(second, column[OWNERS:], 0.0))

    slots, scales = placed(slots), placed(scales)
    row = iota((ROWS, LANES), 0)
    at = 2 * lax.div(q, 2)
    for o in range(OWNERS):
        tile = jnp.where(row == at, slots[o : o + 1], jnp.where(row == at + 1, scales[o : o + 1], 0.0))
        sendz[o, 2] = tile.astype(BF16)


def move_blocks(choose, raw, sendz):
    count = raw.shape[0]
    data = raw[...].reshape(count * ROWS, LANES)
    chosen = jnp.dot(choose[...], data, preferred_element_type=F32).astype(BF16).reshape(PAIR, OWNERS, ROWS, LANES)
    for k in range(PAIR):
        sendz[:, k] = chosen[k]


def kernel(
    capacity, scale_hbm, held_hbm, dest_hbm, deltas_ref, old_ref, out_ref,
    scale_ref, held_ref, dest_ref, note, raw, notes, choose, sendz, grid, metas, weights, old, in_sem, old_sem, small_sem,
    send1, recv1, send2, recv2, send3, recv3, send4, recv4, send5, recv5, send6, recv6, send7, recv7, send8, recv8, ready, go,
):
    f, e = lax.axis_index("fsdp"), lax.axis_index("expert")
    y, r = lax.div(f, CHUNKS), lax.rem(f, CHUNKS)
    x, core = lax.div(r, 2), lax.rem(r, 2)
    half = lax.rem(e, 2)
    collects = y == home(e)
    base = lax.rem(y + 4, ALONG_Y) * 2
    count = CHUNKS * ALONG_Y

    def where(to_f, to_e):
        return dict(device_id={"fsdp": to_f, "expert": to_e}, device_id_type=pl.DeviceIdType.MESH)

    def remote(src, dst, send, recv, to_f, to_e):
        return pltpu.make_async_remote_copy(
            src_ref=src, dst_ref=dst, send_sem=send, recv_sem=recv, **where(to_f, to_e)
        )

    def wait_bytes(ref, sem):
        pltpu.make_async_copy(ref, ref, sem).wait()

    small = [
        pltpu.make_async_copy(src, dst, small_sem.at[i])
        for i, (src, dst) in enumerate([(scale_hbm, scale_ref), (held_hbm, held_ref), (dest_hbm, dest_ref)])
    ]
    for copy in small:
        copy.start()

    barrier = pltpu.get_barrier_semaphore()

    def greet(to_f, to_e):
        pl.semaphore_signal(barrier, inc=1, **where(to_f, to_e))

    @pl.when(collects)
    def _():
        for d in FAR_FIRST + (0,):
            for shift in range(d == 0, CHUNKS):
                greet(lax.rem(y + d, ALONG_Y) * CHUNKS + lax.rem(r + shift, CHUNKS), e)
        for plane in range(1, OWNERS):
            pl.when(plane > e)(functools.partial(greet, f, plane))

    sibling = y * CHUNKS + x * 2 + (1 - core)

    for h in range(2):
        pl.when(e < base + h)(functools.partial(greet, f, base + h))

    for copy in small:
        copy.wait()
    note[...] = own_meta(f, scale_ref, held_ref, dest_ref)

    lower = (base < e).astype(jnp.int32) + (base + 1 < e).astype(jnp.int32)
    pl.semaphore_wait(barrier, lower + jnp.where(collects, CHUNKS - 1 + e, CHUNKS))
    for h in range(2):
        def answer(h=h):
            pl.semaphore_signal(ready, inc=1, **where(f, base + h))
        pl.when(base + h < e)(answer)

    for shift in FAR_FIRST + (0,):
        i = lax.rem(r + shift, CHUNKS)

        def send_note(i=i):
            remote(note, notes.at[f], send8, recv8, home(e) * CHUNKS + i, e).start()
        pl.when(jnp.logical_not(collects))(send_note) if shift == 0 else send_note()
    for shift in FAR_FIRST + (0,):
        i = lax.rem(r + shift, CHUNKS)

        def send_chunk(i=i):
            remote(deltas_ref.at[i], raw.at[f], send1, recv1, home(e) * CHUNKS + i, e).start()
        pl.when(jnp.logical_not(collects))(send_chunk) if shift == 0 else send_chunk()
    fetch_old = pltpu.make_async_copy(old_ref, old, old_sem)
    fetch_old.start()

    @pl.when(collects)
    def _():
        own_chunk = pltpu.make_async_copy(deltas_ref.at[r], raw.at[f], in_sem)
        own_chunk.start()
        notes[f] = note[...]
        own_chunk.wait()
        wait_bytes(notes.at[pl.ds(0, count - 1)], recv8)
        plan_blocks(e, capacity, notes, choose, sendz)
        wait_bytes(raw.at[pl.ds(0, count - 1)], recv1)
        move_blocks(choose, raw, sendz)
        mine = pl.ds(y * PIECE + half * PAIR, PAIR)
        place = y * 2 + half

        def along_z(plane):
            remote(sendz.at[plane, pl.ds(0, PAIR)], grid.at[r, mine], send2, recv2.at[half], f, plane).start()
            remote(sendz.at[plane, PAIR], metas.at[place], send3, recv3.at[half], f, plane).start()

        for plane in range(OWNERS - 1):
            pl.when(plane < e)(functools.partial(along_z, plane))
        grid[r, mine] = sendz[e, pl.ds(0, PAIR)]
        metas[place] = sendz[e, PAIR]
        for d in FAR_FIRST:
            pl.semaphore_signal(go, inc=1, **where(lax.rem(f + d * CHUNKS, count), e))
        pl.when(e < OWNERS - 1)(lambda: pl.semaphore_wait(ready, OWNERS - 1 - e))
        for plane in range(1, OWNERS):
            pl.when(plane > e)(functools.partial(along_z, plane))

    pl.when(jnp.logical_not(collects))(lambda: pl.semaphore_wait(go, 1))

    def along_x(row):
        part = grid.at[r, pl.ds(row * PIECE, PIECE)]
        for d in (2, 1, 3):
            remote(part, part, send5, recv5.at[d - 1], y * CHUNKS + lax.rem(r + 2 * d, CHUNKS), e).start()

    def own_piece():
        for h in range(2):
            def arrive(h=h):
                wait_bytes(grid.at[r, pl.ds(y * PIECE + h * PAIR, PAIR)], recv2.at[h])
                wait_bytes(metas.at[y * 2 + h], recv3.at[h])
            pl.when(jnp.logical_not(collects & (half == h)))(arrive)
        part, both = grid.at[r, pl.ds(y * PIECE, PIECE)], metas.at[pl.ds(y * 2, 2)]
        for d in FAR_FIRST:
            remote(part, part, send4, recv4.at[y], lax.rem(f + d * CHUNKS, count), e).start()
        along_x(y)
        for d in FAR_FIRST:
            remote(both, both, send7, recv7, lax.rem(f + d * CHUNKS, count), e).start()

    def other_piece(row):
        def arrive():
            wait_bytes(grid.at[r, pl.ds(row * PIECE, PIECE)], recv4.at[row])
            along_x(row)
        pl.when(y != row)(arrive)

    pl.when(y >= 4)(own_piece)
    for row in (5, 4, 6):
        other_piece(row)
    pl.when(y < 4)(own_piece)
    for row in (7, 0, 1, 2, 3):
        other_piece(row)

    remote(grid.at[r], grid.at[r], send6, recv6.at[0], sibling, e).start()
    wait_bytes(metas.at[pl.ds(0, 2 * (ALONG_Y - 1))], recv7)
    total = jnp.sum(metas[...].astype(F32), axis=0)
    slots = jnp.concatenate([total[2 * g : 2 * g + 1] for g in range(4)], axis=1)
    scales = jnp.concatenate([total[2 * g + 1 : 2 * g + 2] for g in range(4)], axis=1)
    deep = 4 * LANES
    target = (slots.astype(jnp.int32) - 1) * ROWS + iota((1, deep), 1) % ROWS
    tall = capacity * ROWS
    weights[...] = jnp.where(iota((tall, deep), 0) == target, scales, 0.0).astype(BF16)
    fetch_old.wait()

    def add(i):
        values = grid[i].reshape(deep, LANES)
        update = jnp.dot(weights[...], values, preferred_element_type=F32)
        new = old[:, i].astype(F32) + update.reshape(capacity, ROWS, LANES)
        out_ref[:, i] = new.astype(BF16)

    add(r)
    for d in (1, 3, 2):
        src = lax.rem(r + CHUNKS - 2 * d, CHUNKS)
        wait_bytes(grid.at[src], recv5.at[d - 1])
        remote(grid.at[src], grid.at[src], send6, recv6.at[d], sibling, e).start()
    for d in (1, 3, 2):
        add(lax.rem(r + CHUNKS - 2 * d, CHUNKS))
    for d in (0, 1, 3, 2):
        src = lax.rem(r + CHUNKS - 2 * d, CHUNKS) + 1 - 2 * core
        wait_bytes(grid.at[src], recv6.at[d])
        add(src)

    wait_bytes(grid.at[r, pl.ds(0, PIECE * (ALONG_Y - 1))], send4)
    wait_bytes(metas.at[pl.ds(0, 2 * (ALONG_Y - 1))], send7)
    wait_bytes(grid.at[pl.ds(0, 3)], send5)
    wait_bytes(grid.at[pl.ds(0, 4)], send6)

    @pl.when(collects)
    def _():
        wait_bytes(grid.at[r, pl.ds(0, PAIR * (OWNERS - 1))], send2)
        wait_bytes(metas.at[pl.ds(0, OWNERS - 1)], send3)
        wait_bytes(raw.at[pl.ds(0, CHUNKS - 1)], send1)
        wait_bytes(notes.at[pl.ds(0, CHUNKS - 1)], send8)

    @pl.when(jnp.logical_not(collects))
    def _():
        wait_bytes(raw.at[pl.ds(0, CHUNKS)], send1)
        wait_bytes(notes.at[pl.ds(0, CHUNKS)], send8)


def near(array):
    return pltpu.with_memory_space_constraint(array, pltpu.HBM)


def shards(deltas, scales, held_block, block_dest, rollout_old):
    capacity, size = rollout_old.shape[0], rollout_old.shape[1]
    count = CHUNKS * ALONG_Y
    dma, vmem = pltpu.SemaphoreType.DMA, pltpu.VMEM
    out = pl.pallas_call(
        functools.partial(kernel, capacity),
        out_shape=jax.ShapeDtypeStruct((capacity, CHUNKS, ROWS, LANES), BF16),
        in_specs=[
            pl.BlockSpec(memory_space=pltpu.HBM),
            pl.BlockSpec(memory_space=pltpu.HBM),
            pl.BlockSpec(memory_space=pltpu.HBM),
            pl.BlockSpec(memory_space=pltpu.HBM),
            pl.BlockSpec(memory_space=pltpu.HBM),
        ],
        out_specs=pl.BlockSpec(memory_space=pltpu.VMEM),
        scratch_shapes=[
            vmem((1,), BF16), pltpu.SMEM((1,), jnp.int32), pltpu.SMEM(block_dest.shape, jnp.int32),
            vmem((1, LANES), F32),
            vmem((count, ROWS, LANES), BF16),
            vmem((count, 1, LANES), F32),
            vmem((PAIR * OWNERS * ROWS, count * ROWS), BF16),
            vmem((OWNERS, PAIR + 1, ROWS, LANES), BF16),
            vmem((CHUNKS, TILES, ROWS, LANES), BF16),
            vmem((OWNERS, ROWS, LANES), BF16),
            vmem((capacity * ROWS, 4 * LANES), BF16),
            vmem((capacity, CHUNKS, ROWS, LANES), BF16),
            dma, dma, dma((3,)),
            dma, dma,
            dma, dma((2,)),
            dma, dma((2,)),
            dma, dma((ALONG_Y,)),
            dma, dma((3,)),
            dma, dma((4,)),
            dma, dma,
            dma, dma,
            pltpu.SemaphoreType.REGULAR,
            pltpu.SemaphoreType.REGULAR,
        ],
        compiler_params=pltpu.CompilerParams(
            collective_id=1, has_side_effects=True, vmem_limit_bytes=40 * 1024 * 1024
        ),
    )(
        scales,
        held_block,
        near(block_dest),
        near(deltas.reshape(CHUNKS, ROWS, LANES)),
        near(rollout_old.reshape(capacity, CHUNKS, ROWS, LANES)),
    )
    return out.reshape(capacity, size, size)


def solution(mesh):
    in_specs = (
        P(("fsdp", "expert"), None, None),
        P(("fsdp", "expert")),
        P(("fsdp", "expert")),
        P(),
        P("expert", None, None),
    )
    return jax.shard_map(shards, mesh=mesh, in_specs=in_specs, out_specs=P("expert", None, None), check_vma=False)
```

```python
import functools

import jax
import jax.numpy as jnp
from jax import lax
from jax.experimental import pallas as pl
from jax.experimental.pallas import tpu as pltpu
from jax.sharding import PartitionSpec as P

ROWS = 16
LANES = 128
CHUNKS = 8
ALONG_Y = 8
OWNERS = 16
PAIR = 2
PIECE = 2 * PAIR
TILES = ALONG_Y * PIECE
FAR_FIRST = (4, 3, 5, 2, 6, 1, 7)
F32 = jnp.float32
BF16 = jnp.bfloat16


def home(e):
    pair = lax.div(e, 2)
    return jnp.where(pair < 4, pair + 3, jnp.where(pair < 7, pair - 4, 7))


def iota(shape, dim):
    return lax.broadcasted_iota(jnp.int32, shape, dim)


def own_meta(f, scale_ref, held_ref, dest_ref):
    held = held_ref[0]
    dest = jnp.where(held >= 0, dest_ref[jnp.maximum(held, 0)] + 1, 0).astype(F32)
    scale = jnp.broadcast_to(scale_ref[...].astype(F32).reshape(1, 1), (1, LANES))
    lane = iota((1, LANES), 1)
    return jnp.where(lane == f, dest, jnp.where(lane == f + LANES // 2, scale, 0.0))


def plan_blocks(e, capacity, notes, choose, sendz):
    count = notes.shape[0]
    total = jnp.sum(notes[...], axis=0)
    scale = jnp.concatenate([total[:, LANES // 2 :], total[:, : LANES // 2]], axis=1)
    held = (iota((1, LANES), 1) < LANES // 2) & (total > 0.0)
    whole = jnp.floor((total - 0.5) * (1.0 / capacity))
    owner = jnp.where(held, whole + 1.0, 0.0)
    slot = jnp.where(held, total - whole * capacity, 0.0)
    onehot = (iota((OWNERS, LANES), 0).astype(F32) + 1.0 == owner).astype(F32)
    earlier = (iota((LANES, LANES), 0) < iota((LANES, LANES), 1)).astype(F32).astype(BF16)
    before = jnp.dot(onehot.astype(BF16), earlier, preferred_element_type=F32)
    rank = jnp.sum(onehot * before, axis=0, keepdims=True)
    place = jnp.where(owner > 0.0, rank * OWNERS + owner - 1.0, -64.0)
    wide = count * ROWS
    spread = (iota((LANES, wide), 0) == iota((LANES, wide), 1) // ROWS).astype(F32).astype(BF16)
    places = jnp.dot(jnp.broadcast_to(place, (8, LANES)).astype(BF16), spread, preferred_element_type=F32)[0:1]
    target = places.astype(jnp.int32) * ROWS + iota((1, wide), 1) % ROWS
    tall = PAIR * OWNERS * ROWS
    choose[...] = (iota((tall, wide), 0) == target).astype(F32).astype(BF16)
    mine = iota((PAIR * OWNERS, LANES), 0).astype(F32) == place
    slots = jnp.sum(jnp.where(mine, slot, 0.0), axis=1, keepdims=True)
    scales = jnp.sum(jnp.where(mine, scale, 0.0), axis=1, keepdims=True)
    lane = iota((OWNERS, LANES), 1)
    q, half = home(e), lax.rem(e, 2)
    start = lax.rem(q, 2) * 64 + half * 32
    first = (lane >= start) & (lane < start + ROWS)
    second = (lane >= start + ROWS) & (lane < start + 2 * ROWS)

    def placed(column):
        return jnp.where(first, column[:OWNERS], jnp.where(second, column[OWNERS:], 0.0))

    slots, scales = placed(slots), placed(scales)
    row = iota((ROWS, LANES), 0)
    at = 2 * lax.div(q, 2)
    for o in range(OWNERS):
        tile = jnp.where(row == at, slots[o : o + 1], jnp.where(row == at + 1, scales[o : o + 1], 0.0))
        sendz[o, 2] = tile.astype(BF16)


def move_blocks(choose, raw, sendz):
    count = raw.shape[0]
    data = raw[...].reshape(count * ROWS, LANES)
    chosen = jnp.dot(choose[...], data, preferred_element_type=F32).astype(BF16).reshape(PAIR, OWNERS, ROWS, LANES)
    for k in range(PAIR):
        sendz[:, k] = chosen[k]


def kernel(
    capacity, scale_hbm, held_hbm, dest_hbm, deltas_ref, old_ref, out_ref,
    scale_ref, held_ref, dest_ref, note, raw, notes, choose, sendz, grid, metas, weights, old, in_sem, old_sem, small_sem,
    send1, recv1, send2, recv2, send3, recv3, send4, recv4, send5, recv5, send6, recv6, send7, recv7, send8, recv8, ready, go,
):
    f, e = lax.axis_index("fsdp"), lax.axis_index("expert")
    y, r = lax.div(f, CHUNKS), lax.rem(f, CHUNKS)
    x, core = lax.div(r, 2), lax.rem(r, 2)
    half = lax.rem(e, 2)
    collects = y == home(e)
    base = 2 * jnp.where(y < 3, y + 4, jnp.where(y < 7, y - 3, 7))
    early = (y >= 3) & (y < 7)
    count = CHUNKS * ALONG_Y

    def where(to_f, to_e):
        return dict(device_id={"fsdp": to_f, "expert": to_e}, device_id_type=pl.DeviceIdType.MESH)

    def remote(src, dst, send, recv, to_f, to_e):
        return pltpu.make_async_remote_copy(
            src_ref=src, dst_ref=dst, send_sem=send, recv_sem=recv, **where(to_f, to_e)
        )

    def wait_bytes(ref, sem):
        pltpu.make_async_copy(ref, ref, sem).wait()

    small = [
        pltpu.make_async_copy(src, dst, small_sem.at[i])
        for i, (src, dst) in enumerate([(scale_hbm, scale_ref), (held_hbm, held_ref), (dest_hbm, dest_ref)])
    ]
    for copy in small:
        copy.start()

    barrier = pltpu.get_barrier_semaphore()

    def greet(to_f, to_e):
        pl.semaphore_signal(barrier, inc=1, **where(to_f, to_e))

    @pl.when(collects)
    def _():
        for d in FAR_FIRST + (0,):
            for shift in range(d == 0, CHUNKS):
                greet(lax.rem(y + d, ALONG_Y) * CHUNKS + lax.rem(r + shift, CHUNKS), e)
        for plane in range(1, OWNERS):
            pl.when(plane > e)(functools.partial(greet, f, plane))

    sibling = y * CHUNKS + x * 2 + (1 - core)

    for h in range(2):
        pl.when(e < base + h)(functools.partial(greet, f, base + h))

    for copy in small:
        copy.wait()
    note[...] = own_meta(f, scale_ref, held_ref, dest_ref)

    lower = (base < e).astype(jnp.int32) + (base + 1 < e).astype(jnp.int32)
    pl.semaphore_wait(barrier, lower + jnp.where(collects, CHUNKS - 1 + e, CHUNKS))
    for h in range(2):
        def answer(h=h):
            pl.semaphore_signal(ready, inc=1, **where(f, base + h))
        pl.when(base + h < e)(answer)

    for shift in FAR_FIRST + (0,):
        i = lax.rem(r + shift, CHUNKS)

        def send_note(i=i):
            remote(note, notes.at[f], send8, recv8, home(e) * CHUNKS + i, e).start()
        pl.when(jnp.logical_not(collects))(send_note) if shift == 0 else send_note()
    for shift in FAR_FIRST + (0,):
        i = lax.rem(r + shift, CHUNKS)

        def send_chunk(i=i):
            remote(deltas_ref.at[i], raw.at[f], send1, recv1, home(e) * CHUNKS + i, e).start()
        pl.when(jnp.logical_not(collects))(send_chunk) if shift == 0 else send_chunk()
    fetch_old = pltpu.make_async_copy(old_ref, old, old_sem)
    fetch_old.start()

    @pl.when(collects)
    def _():
        own_chunk = pltpu.make_async_copy(deltas_ref.at[r], raw.at[f], in_sem)
        own_chunk.start()
        notes[f] = note[...]
        own_chunk.wait()
        wait_bytes(notes.at[pl.ds(0, count - 1)], recv8)
        plan_blocks(e, capacity, notes, choose, sendz)
        wait_bytes(raw.at[pl.ds(0, count - 1)], recv1)
        move_blocks(choose, raw, sendz)
        mine = pl.ds(y * PIECE + half * PAIR, PAIR)
        place = y * 2 + half

        def along_z(plane):
            remote(sendz.at[plane, pl.ds(0, PAIR)], grid.at[r, mine], send2, recv2.at[half], f, plane).start()
            remote(sendz.at[plane, PAIR], metas.at[place], send3, recv3.at[half], f, plane).start()

        for plane in range(OWNERS - 1):
            pl.when(plane < e)(functools.partial(along_z, plane))
        grid[r, mine] = sendz[e, pl.ds(0, PAIR)]
        metas[place] = sendz[e, PAIR]
        for d in FAR_FIRST:
            pl.semaphore_signal(go, inc=1, **where(lax.rem(f + d * CHUNKS, count), e))
        pl.when(e < OWNERS - 1)(lambda: pl.semaphore_wait(ready, OWNERS - 1 - e))
        for plane in range(1, OWNERS):
            pl.when(plane > e)(functools.partial(along_z, plane))

    pl.when(jnp.logical_not(collects))(lambda: pl.semaphore_wait(go, 1))

    def along_x(row):
        part = grid.at[r, pl.ds(row * PIECE, PIECE)]
        for d in (2, 1, 3):
            remote(part, part, send5, recv5.at[d - 1], y * CHUNKS + lax.rem(r + 2 * d, CHUNKS), e).start()

    def own_piece():
        for h in range(2):
            def arrive(h=h):
                wait_bytes(grid.at[r, pl.ds(y * PIECE + h * PAIR, PAIR)], recv2.at[h])
                wait_bytes(metas.at[y * 2 + h], recv3.at[h])
            pl.when(jnp.logical_not(collects & (half == h)))(arrive)
        part, both = grid.at[r, pl.ds(y * PIECE, PIECE)], metas.at[pl.ds(y * 2, 2)]
        for d in FAR_FIRST:
            remote(part, part, send4, recv4.at[y], lax.rem(f + d * CHUNKS, count), e).start()
        along_x(y)
        for d in FAR_FIRST:
            remote(both, both, send7, recv7, lax.rem(f + d * CHUNKS, count), e).start()

    def other_piece(row):
        def arrive():
            wait_bytes(grid.at[r, pl.ds(row * PIECE, PIECE)], recv4.at[row])
            along_x(row)
        pl.when(y != row)(arrive)

    pl.when(early)(own_piece)
    for row in (4, 3, 5):
        other_piece(row)
    pl.when(jnp.logical_not(early))(own_piece)
    for row in (6, 0, 1, 2, 7):
        other_piece(row)

    remote(grid.at[r], grid.at[r], send6, recv6.at[0], sibling, e).start()
    wait_bytes(metas.at[pl.ds(0, 2 * (ALONG_Y - 1))], recv7)
    total = jnp.sum(metas[...].astype(F32), axis=0)
    slots = jnp.concatenate([total[2 * g : 2 * g + 1] for g in range(4)], axis=1)
    scales = jnp.concatenate([total[2 * g + 1 : 2 * g + 2] for g in range(4)], axis=1)
    deep = 4 * LANES
    target = (slots.astype(jnp.int32) - 1) * ROWS + iota((1, deep), 1) % ROWS
    tall = capacity * ROWS
    weights[...] = jnp.where(iota((tall, deep), 0) == target, scales, 0.0).astype(BF16)
    fetch_old.wait()

    def add(i):
        values = grid[i].reshape(deep, LANES)
        update = jnp.dot(weights[...], values, preferred_element_type=F32)
        new = old[:, i].astype(F32) + update.reshape(capacity, ROWS, LANES)
        out_ref[:, i] = new.astype(BF16)

    add(r)
    for d in (1, 3, 2):
        src = lax.rem(r + CHUNKS - 2 * d, CHUNKS)
        wait_bytes(grid.at[src], recv5.at[d - 1])
        remote(grid.at[src], grid.at[src], send6, recv6.at[d], sibling, e).start()
    for d in (1, 3, 2):
        add(lax.rem(r + CHUNKS - 2 * d, CHUNKS))
    for d in (0, 1, 3, 2):
        src = lax.rem(r + CHUNKS - 2 * d, CHUNKS) + 1 - 2 * core
        wait_bytes(grid.at[src], recv6.at[d])
        add(src)

    wait_bytes(grid.at[r, pl.ds(0, PIECE * (ALONG_Y - 1))], send4)
    wait_bytes(metas.at[pl.ds(0, 2 * (ALONG_Y - 1))], send7)
    wait_bytes(grid.at[pl.ds(0, 3)], send5)
    wait_bytes(grid.at[pl.ds(0, 4)], send6)

    @pl.when(collects)
    def _():
        wait_bytes(grid.at[r, pl.ds(0, PAIR * (OWNERS - 1))], send2)
        wait_bytes(metas.at[pl.ds(0, OWNERS - 1)], send3)
        wait_bytes(raw.at[pl.ds(0, CHUNKS - 1)], send1)
        wait_bytes(notes.at[pl.ds(0, CHUNKS - 1)], send8)

    @pl.when(jnp.logical_not(collects))
    def _():
        wait_bytes(raw.at[pl.ds(0, CHUNKS)], send1)
        wait_bytes(notes.at[pl.ds(0, CHUNKS)], send8)


def near(array):
    return pltpu.with_memory_space_constraint(array, pltpu.HBM)


def shards(deltas, scales, held_block, block_dest, rollout_old):
    capacity, size = rollout_old.shape[0], rollout_old.shape[1]
    count = CHUNKS * ALONG_Y
    dma, vmem = pltpu.SemaphoreType.DMA, pltpu.VMEM
    out = pl.pallas_call(
        functools.partial(kernel, capacity),
        out_shape=jax.ShapeDtypeStruct((capacity, CHUNKS, ROWS, LANES), BF16),
        in_specs=[
            pl.BlockSpec(memory_space=pltpu.HBM),
            pl.BlockSpec(memory_space=pltpu.HBM),
            pl.BlockSpec(memory_space=pltpu.HBM),
            pl.BlockSpec(memory_space=pltpu.HBM),
            pl.BlockSpec(memory_space=pltpu.HBM),
        ],
        out_specs=pl.BlockSpec(memory_space=pltpu.VMEM),
        scratch_shapes=[
            vmem((1,), BF16), pltpu.SMEM((1,), jnp.int32), pltpu.SMEM(block_dest.shape, jnp.int32),
            vmem((1, LANES), F32),
            vmem((count, ROWS, LANES), BF16),
            vmem((count, 1, LANES), F32),
            vmem((PAIR * OWNERS * ROWS, count * ROWS), BF16),
            vmem((OWNERS, PAIR + 1, ROWS, LANES), BF16),
            vmem((CHUNKS, TILES, ROWS, LANES), BF16),
            vmem((OWNERS, ROWS, LANES), BF16),
            vmem((capacity * ROWS, 4 * LANES), BF16),
            vmem((capacity, CHUNKS, ROWS, LANES), BF16),
            dma, dma, dma((3,)),
            dma, dma,
            dma, dma((2,)),
            dma, dma((2,)),
            dma, dma((ALONG_Y,)),
            dma, dma((3,)),
            dma, dma((4,)),
            dma, dma,
            dma, dma,
            pltpu.SemaphoreType.REGULAR,
            pltpu.SemaphoreType.REGULAR,
        ],
        compiler_params=pltpu.CompilerParams(
            collective_id=1, has_side_effects=True, vmem_limit_bytes=40 * 1024 * 1024
        ),
    )(
        scales,
        held_block,
        near(block_dest),
        near(deltas.reshape(CHUNKS, ROWS, LANES)),
        near(rollout_old.reshape(capacity, CHUNKS, ROWS, LANES)),
    )
    return out.reshape(capacity, size, size)


def solution(mesh):
    in_specs = (
        P(("fsdp", "expert"), None, None),
        P(("fsdp", "expert")),
        P(("fsdp", "expert")),
        P(),
        P("expert", None, None),
    )
    return jax.shard_map(shards, mesh=mesh, in_specs=in_specs, out_specs=P("expert", None, None), check_vma=False)
```
